256 devices in a mesh: island: 8 (over z_lo, core), fsdp: 32 (over z_hi, y, x).
Axes of the slice: x: 4, y: 4, z: 8 (z_hi: 2, z_lo: 4; z = z_hi * 4 + z_lo), core: 2. Of those that a mesh axis runs over, the one named last changes fastest.
Arguments:
- activations: bfloat16 [8, 32768, 5120], P('island', 'fsdp'), may hold values from -6 to 6
- upstream: bfloat16 [8, 32768, 384], P('island', 'fsdp'), may hold values from -0.0625 to 0.0625
- drift: float32 [8, 384, 5120], P('island', 'fsdp'), may hold values from -0.75 to 0.75
- first_moment: float32 [8, 384, 5120], P('island', 'fsdp'), may hold values from -4 to 4
- second_moment: float32 [8, 384, 5120], P('island', 'fsdp'), may hold values from 0.01 to 1
- outer_base: float32 [384, 5120], P('fsdp'), may hold values from -0.3 to 0.3
- outer_momentum: float32 [384, 5120], P('fsdp'), may hold values from -0.75 to 0.75
- scale_exponents: int32 [384, 40], P('fsdp'), may hold values from -12 to -5
Outputs:
- first_new: float32 [8, 384, 5120], P('island', 'fsdp')
- second_new: float32 [8, 384, 5120], P('island', 'fsdp')
- momentum_new: float32 [384, 5120], P('fsdp', 'island')
- base_new: float32 [384, 5120], P('fsdp', 'island')
- fragment: bfloat16 [384, 5120], replicated
The draws below stay inside these ranges and needn't reach their ends.
All inputs are finite; a program needn't handle non-finite values.
Results may differ from the reference program's by a relative error of at most 0.015.
Values may be sent and summed in bfloat16 or wider, within the bound.
No kernel may reach another device: no remote copies, remote signals or barrier semaphores. Data moves between devices by JAX's collectives and lax.ppermute only.
A program may use at most 64 MiB of HBM per device.

```python
import math
import jax
import jax.numpy as jnp
from jax import lax

D = 5120
BLOCK = 128
TOK_DEV = 1024
ROWS = 384
TOK_ISL = 32768
N_ISLAND = 8
N_FSDP = 32


def draw_outer_base(key, part):
    key = jax.random.fold_in(key, 11)
    values = jnp.clip(0.05 * jax.random.normal(key, (ROWS, D), jnp.float32), -0.3, 0.3)
    return values


def touch_ends(entries, stream_key, smallest, high):
    dims = entries.shape
    place = [jax.random.randint(jax.random.fold_in(stream_key, axis), (), 0, dims[axis]) for axis in range(len(dims))]
    entries = entries.at[tuple(place)].set(smallest)
    longest = dims.index(max(dims))
    place[longest] = (place[longest] + 1) % dims[longest]
    return entries.at[tuple(place)].set(high)


def strengthened(entries, key, source, target, blocks, factor):
    owner, partner = [(jnp.arange(entries.shape[axis_at]) // (entries.shape[axis_at] // blocks)).reshape([-1 if axis == axis_at else 1 for axis in range(entries.ndim)]) for axis_at in (source, target)]
    chosen = jax.random.permutation(key, blocks)[partner]
    strong = (owner == chosen) | (owner == (partner + blocks // 2) % blocks)
    return jnp.where(strong, factor * entries, entries)


def level_of(key, extent, cuts, least, top_value):
    gain, own = 1.0, jax.random.fold_in(key, 6)
    for position, shards_of in cuts:
        steps = jnp.exp(jax.random.uniform(jax.random.fold_in(own, position), (shards_of,), jnp.float32, least / len(cuts), top_value / len(cuts)))
        gain = gain * jnp.repeat(steps, extent[position] // shards_of).reshape([-1 if axis == position else 1 for axis in range(len(extent))])
    return gain


def normal_values(stream_key, shape, spread, reach, split=(), held_as=jnp.bfloat16):
    result = spread * jax.random.normal(stream_key, shape, jnp.float32)
    if split:
        result = result * level_of(stream_key, shape, split, -0.22, 0.18)
    return jnp.clip(result, -reach, reach).astype(held_as)


def gaussian_with(own_key, extent, spread, most, split, heavy, held_as=jnp.bfloat16):
    result = spread * jax.random.normal(own_key, extent, jnp.float32)
    if split:
        result = result * level_of(own_key, extent, split, -0.22, 0.18)
    return jnp.clip(strengthened(result, jax.random.fold_in(own_key, 3), *heavy), -most, most).astype(held_as)


def setup_inputs(seed: int = 0) -> dict:
    keys = jax.random.split(jax.random.key(seed), 9)
    return {
        "activations": normal_values(keys[0], (N_ISLAND, TOK_ISL, D), 1.0, 6.0, ((0, 8), (1, 32))),
        "upstream": gaussian_with(keys[1], (N_ISLAND, TOK_ISL, ROWS), TOK_ISL ** -0.5, 0.0625, ((0, 8), (1, 32)), (1, 2, 32, 2.75)),
        "drift": normal_values(keys[2], (N_ISLAND, ROWS, D), 0.05, 0.75, ((0, 8), (1, 32)), jnp.float32),
        "first_moment": normal_values(keys[3], (N_ISLAND, ROWS, D), 0.3, 4.0, ((0, 8), (1, 32)), jnp.float32),
        "second_moment": jnp.clip(jnp.exp(math.log(1.0) - 4.6051702 * jax.random.uniform(keys[4], (N_ISLAND, ROWS, D), jnp.float32) ** level_of(keys[4], (N_ISLAND, ROWS, D), ((0, 8), (1, 32)), -0.2, 0.2)), 0.01, 1.0),
        "outer_base": draw_outer_base(jax.random.fold_in(keys[8], 71), 0),
        "outer_momentum": normal_values(keys[6], (ROWS, D), 0.05, 0.75, ((0, 32),), jnp.float32),
        "scale_exponents": touch_ends(jax.random.randint(keys[7], (ROWS, D // BLOCK), -12, -4), jax.random.fold_in(keys[7], 1), -12, (-4) - 1).astype(jnp.int32),
    }


INNER_RATE = 0.02
OUTER_RATE = 0.7
BETA_FIRST = 0.9
BETA_SECOND = 0.95
CORRECT_FIRST = 1.0 - 0.9 ** 10
CORRECT_SECOND = 1.0 - 0.95 ** 10
WEIGHT_DECAY = 0.1
EPSILON = 1e-08
NESTEROV_MU = 0.9

def island_gradient(inputs):
    features, upstream_rows = inputs
    features = features.reshape(N_FSDP, TOK_DEV, D)
    upstream_rows = upstream_rows.reshape(N_FSDP, TOK_DEV, ROWS)

    def add_group(running, group):
        group_feat, group_up = group
        partial_value = jnp.dot(group_up.T, group_feat, preferred_element_type=jnp.float32).astype(jnp.bfloat16)
        return (running + partial_value.astype(jnp.float32), None)
    summed, unused = lax.scan(add_group, jnp.zeros((ROWS, D), jnp.float32), (features, upstream_rows))
    return summed

def reference(activations, upstream, drift, first_moment, second_moment, outer_base, outer_momentum, scale_exponents):
    gradient = lax.map(island_gradient, (activations, upstream))
    params = outer_base[None] + drift
    first_new = BETA_FIRST * first_moment + (1.0 - BETA_FIRST) * gradient
    second_new = BETA_SECOND * second_moment + (1.0 - BETA_SECOND) * gradient * gradient
    update = first_new / CORRECT_FIRST / (jnp.sqrt(second_new / CORRECT_SECOND) + EPSILON) + WEIGHT_DECAY * params
    inner = params - INNER_RATE * update
    delta = outer_base[None] - inner
    exponent_f = jnp.repeat(scale_exponents, BLOCK, axis=1).astype(jnp.float32)
    scaling = jnp.exp2(-exponent_f)
    unscale = jnp.exp2(exponent_f)
    coded = jnp.clip(delta * scaling[None], -127.0, 127.0)
    summed = lax.optimization_barrier(jnp.sum(coded, axis=0))
    pseudo = summed * unscale / N_ISLAND
    momentum_new = NESTEROV_MU * outer_momentum + pseudo
    base_new = outer_base - OUTER_RATE * (pseudo + NESTEROV_MU * momentum_new)
    fragment = base_new.astype(jnp.bfloat16)
    return (first_new, second_new, momentum_new, base_new, fragment)
```

```python
import functools

import jax
import jax.numpy as jnp
import numpy as np
from jax import lax
from jax.experimental import pallas as pl
from jax.experimental.pallas import tpu as pltpu
from jax.sharding import PartitionSpec as P

INNER_RATE = 0.02
OUTER_RATE = 0.7
BETA_FIRST = 0.9
BETA_SECOND = 0.95
CORRECT_FIRST = 1.0 - 0.9**10
CORRECT_SECOND = 1.0 - 0.95**10
WEIGHT_DECAY = 0.1
EPSILON = 1e-08
NESTEROV_MU = 0.9

N_ISLAND = 8
N_FSDP = 32
N_ZLO = 4
RING = 4
OWN = 12
ROWS = 384
QUARTER = ROWS // 4
PAIR = 2 * OWN
BLOCK = 128
MIB = 1 << 20
BF16 = jnp.bfloat16
F32 = jnp.float32
AXES = ("island", "fsdp")


def device_pairs(target):
    pairs = []
    for zlo in range(N_ZLO):
        for core in range(2):
            for zhi in range(2):
                for y in range(RING):
                    for x in range(RING):
                        here = (zlo, core, zhi, y, x)
                        pairs.append((device_id(*here), device_id(*target(*here))))
    return pairs


def device_id(zlo, core, zhi, y, x):
    return (zlo * 2 + core) * N_FSDP + (zhi * RING + y) * RING + x


def along_a(step):
    def target(zlo, core, zhi, y, x):
        if core == 0:
            return (zlo, core, zhi, y, (x + step) % RING)
        return (zlo, core, zhi, (y + step) % RING, x)

    return device_pairs(target)


def along_b(step):
    def target(zlo, core, zhi, y, x):
        if core == 0:
            return (zlo, core, zhi, (y + step) % RING, x)
        return (zlo, core, zhi, y, (x + step) % RING)

    return device_pairs(target)


OTHER_ZHI = device_pairs(lambda zlo, core, zhi, y, x: (zlo, core, 1 - zhi, y, x))
OTHER_CORE = device_pairs(lambda zlo, core, zhi, y, x: (zlo, 1 - core, zhi, y, x))


def other_zlo(k):
    return device_pairs(lambda zlo, core, zhi, y, x: (zlo ^ k, core, zhi, y, x))


def send(value, pairs):
    return lax.ppermute(value, AXES, pairs)


def fragment_row(position, core, zhi, y, x):
    position = position.astype(F32)
    ja = jnp.floor((position + 0.5) / QUARTER)
    rest = position - QUARTER * ja
    jb = jnp.floor((rest + 0.5) / PAIR)
    rest = rest - PAIR * jb
    jz = jnp.floor((rest + 0.5) / OWN)
    r = rest - OWN * jz
    first = jnp.where(core == 0, ja, jb)
    second = jnp.where(core == 0, jb, ja)
    col = x.astype(F32) + first
    col = jnp.where(col >= RING, col - RING, col)
    line = y.astype(F32) + second
    line = jnp.where(line >= RING, line - RING, line)
    half = jnp.where(zhi == 0, jz, 1.0 - jz)
    return ((half * RING + line) * RING + col) * OWN + r


def product_kernel(pos, up_ref, act_ref, *rest):
    outs, up_rows = rest[:4], rest[4]

    @pl.when(pl.program_id(0) == 0)
    def _():
        _, core, zhi, y, x = (pos[i] for i in range(5))
        wanted = fragment_row(lax.broadcasted_iota(jnp.int32, (ROWS, 1), 0), core, zhi, y, x)
        column = lax.broadcasted_iota(jnp.int32, (ROWS, ROWS), 1).astype(F32)
        pick = jnp.where(column == wanted, 1.0, 0.0).astype(BF16)
        up_rows[...] = lax.dot_general(
            pick, up_ref[...], (((1,), (1,)), ((), ())), preferred_element_type=F32
        ).astype(BF16)

    total = jnp.dot(up_rows[...], act_ref[...], preferred_element_type=F32).astype(BF16)
    for j in range(4):
        outs[j][...] = total[j * QUARTER : (j + 1) * QUARTER]


def product(pos, upstream, activations, first_col, width, tile):
    tokens = activations.shape[1]
    skip = first_col // tile
    return pl.pallas_call(
        product_kernel,
        grid_spec=pltpu.PrefetchScalarGridSpec(
            num_scalar_prefetch=1,
            grid=(width // tile,),
            in_specs=[
                pl.BlockSpec((None, tokens, ROWS), lambda t, p: (0, 0, 0)),
                pl.BlockSpec((None, tokens, tile), lambda t, p: (0, 0, t + skip)),
            ],
            out_specs=[pl.BlockSpec((QUARTER, tile), lambda t, p: (0, t))] * 4,
            scratch_shapes=[pltpu.VMEM((ROWS, tokens), BF16)],
        ),
        out_shape=[jax.ShapeDtypeStruct((QUARTER, width), BF16)] * 4,
        compiler_params=pltpu.CompilerParams(vmem_limit_bytes=32 * MIB),
        cost_estimate=pl.CostEstimate(
            flops=2 * ROWS * tokens * width,
            bytes_accessed=2 * tokens * (width + ROWS) + 2 * ROWS * width,
            transcendentals=0,
        ),
        name="product",
    )(pos, upstream, activations)


def add_first_kernel(own, one, two, three, *outs):
    total = (own[...].astype(F32) + one[...].astype(F32)) + (
        two[...].astype(F32) + three[...].astype(F32)
    )
    for j in range(4):
        outs[j][...] = total[j * PAIR : (j + 1) * PAIR].astype(BF16)


def add_first(parts, tile):
    width = parts[0].shape[1]
    return pl.pallas_call(
        add_first_kernel,
        grid=(width // tile,),
        in_specs=[pl.BlockSpec((QUARTER, tile), lambda t: (0, t))] * 4,
        out_specs=[pl.BlockSpec((PAIR, tile), lambda t: (0, t))] * 4,
        out_shape=[jax.ShapeDtypeStruct((PAIR, width), BF16)] * 4,
        compiler_params=pltpu.CompilerParams(vmem_limit_bytes=32 * MIB),
        name="add_first",
    )(*parts)


def add_second_kernel(own, one, two, three, keep, away):
    total = (own[...].astype(F32) + one[...].astype(F32)) + (
        two[...].astype(F32) + three[...].astype(F32)
    )
    keep[...] = total[:OWN]
    blank = jnp.zeros((16 - OWN, total.shape[1]), F32)
    away[...] = jnp.concatenate([total[OWN:], blank], axis=0).astype(BF16)


def add_second(parts):
    width = parts[0].shape[1]
    return pl.pallas_call(
        add_second_kernel,
        out_shape=[
            jax.ShapeDtypeStruct((OWN, width), F32),
            jax.ShapeDtypeStruct((16, width), BF16),
        ],
        compiler_params=pltpu.CompilerParams(vmem_limit_bytes=32 * MIB),
        name="add_second",
    )(*parts)


def inner_kernel(pos, keep, arrived, drift, first, second, base, exponents, first_out, second_out, own, away, unscale_out):
    core = pos[1]
    width = keep.shape[1]
    share = width // N_ISLAND
    exponent = exponents[...].astype(F32)
    scaling_all = jnp.exp2(-exponent)
    unscale_all = jnp.exp2(exponent)
    per_share = share // BLOCK
    blank = jnp.zeros((16 - OWN, share), F32)
    for i in range(N_ISLAND):
        cols = slice(i * share, (i + 1) * share)
        gradient = keep[:, cols] + arrived[:OWN, cols].astype(F32)
        base_now = base[:, cols]
        params = base_now + drift[:, cols]
        first_new = BETA_FIRST * first[:, cols] + (1.0 - BETA_FIRST) * gradient
        second_new = BETA_SECOND * second[:, cols] + (1.0 - BETA_SECOND) * gradient * gradient
        first_out[:, cols] = first_new
        second_out[:, cols] = second_new
        update = (
            first_new / CORRECT_FIRST / (jnp.sqrt(second_new / CORRECT_SECOND) + EPSILON)
            + WEIGHT_DECAY * params
        )
        inner = params - INNER_RATE * update
        delta = base_now - inner
        blocks = range(i * per_share, (i + 1) * per_share)
        scaling = jnp.concatenate(
            [jnp.broadcast_to(scaling_all[:, b : b + 1], (OWN, BLOCK)) for b in blocks], axis=1
        )
        unscale = jnp.concatenate(
            [jnp.broadcast_to(unscale_all[:, b : b + 1], (OWN, BLOCK)) for b in blocks], axis=1
        )
        coded = jnp.clip(delta * scaling, -127.0, 127.0)
        coded = jnp.concatenate([coded, blank], axis=0).astype(BF16)
        place = slice((i // 2) * share, (i // 2 + 1) * share)

        @pl.when(core == i % 2)
        def _():
            own[:, place] = coded
            unscale_out[:, place] = unscale

        @pl.when(core != i % 2)
        def _():
            away[:, place] = coded


def inner_step(pos, keep, arrived, drift, first, second, base, exponents):
    width = keep.shape[1]
    rows = pl.BlockSpec((None, OWN, width), lambda t, p: (0, 0, 0))

    def whole(a):
        return pl.BlockSpec(a.shape, lambda t, p: (0, 0))

    outs = [
        jax.ShapeDtypeStruct((1, OWN, width), F32),
        jax.ShapeDtypeStruct((1, OWN, width), F32),
        jax.ShapeDtypeStruct((16, width // 2), BF16),
        jax.ShapeDtypeStruct((16, width // 2), BF16),
        jax.ShapeDtypeStruct((OWN, width // 2), F32),
    ]
    return pl.pallas_call(
        inner_kernel,
        grid_spec=pltpu.PrefetchScalarGridSpec(
            num_scalar_prefetch=1,
            grid=(1,),
            in_specs=[whole(keep), whole(arrived), rows, rows, rows, whole(base), whole(exponents)],
            out_specs=[rows, rows] + [whole(o) for o in outs[2:]],
        ),
        out_shape=outs,
        compiler_params=pltpu.CompilerParams(vmem_limit_bytes=32 * MIB),
        name="inner_step",
    )(pos, keep, arrived, drift, first, second, base, exponents)


def add_cores_kernel(own, arrived, out):
    out[...] = (own[...].astype(F32) + arrived[...].astype(F32)).astype(BF16)


def add_cores(own, arrived):
    return pl.pallas_call(
        add_cores_kernel,
        out_shape=jax.ShapeDtypeStruct(own.shape, BF16),
        name="add_cores",
    )(own, arrived)


def outer_kernel(pos, own, one, two, three, unscale, momentum, base, momentum_out, base_out, fragment):
    zlo, core = pos[0], pos[1]
    share = own.shape[1] // N_ZLO
    blank = jnp.zeros((16 - OWN, share), F32)
    for k in range(N_ZLO):
        place = slice(k * share, (k + 1) * share)
        cols = pl.ds(pl.multiple_of((2 * k + core) * share, BLOCK), share)
        summed = (own[:OWN, place].astype(F32) + one[:OWN, place].astype(F32)) + (
            two[:OWN, place].astype(F32) + three[:OWN, place].astype(F32)
        )
        pseudo = summed * unscale[:, place] / N_ISLAND
        momentum_next = NESTEROV_MU * momentum[:, cols] + pseudo
        base_next = base[:, cols] - OUTER_RATE * (pseudo + NESTEROV_MU * momentum_next)
        fragment[:, place] = jnp.concatenate([base_next, blank], axis=0).astype(BF16)

        @pl.when(zlo == k)
        def _():
            momentum_out[...] = momentum_next
            base_out[...] = base_next


def outer_step(pos, parts, unscale, momentum, base):
    width = base.shape[1]
    args = (*parts, unscale, momentum, base)

    def whole(a):
        return pl.BlockSpec(a.shape, lambda t, p: (0, 0))

    outs = [
        jax.ShapeDtypeStruct((OWN, width // N_ISLAND), F32),
        jax.ShapeDtypeStruct((OWN, width // N_ISLAND), F32),
        jax.ShapeDtypeStruct((16, width // 2), BF16),
    ]
    return pl.pallas_call(
        outer_kernel,
        grid_spec=pltpu.PrefetchScalarGridSpec(
            num_scalar_prefetch=1,
            grid=(1,),
            in_specs=[whole(a) for a in args],
            out_specs=[whole(o) for o in outs],
        ),
        out_shape=outs,
        compiler_params=pltpu.CompilerParams(vmem_limit_bytes=32 * MIB),
        name="outer_step",
    )(pos, *args)


def join_pair_kernel(own, arrived, out):
    out[...] = jnp.concatenate(
        [own[:OWN].astype(F32), arrived[:OWN].astype(F32)], axis=0
    ).astype(BF16)


def join_pair(own, arrived):
    return pl.pallas_call(
        join_pair_kernel,
        out_shape=jax.ShapeDtypeStruct((PAIR, own.shape[1]), BF16),
        name="join_pair",
    )(own, arrived)


def join_four_kernel(*refs):
    out = refs[4]
    out[...] = jnp.concatenate([r[...].astype(F32) for r in refs[:4]], axis=0).astype(BF16)


def join_four(parts):
    return pl.pallas_call(
        join_four_kernel,
        out_shape=jax.ShapeDtypeStruct((QUARTER, parts[0].shape[1]), BF16),
        name="join_four",
    )(*parts)


def place_kernel(pos, *refs):
    mine, theirs, out, order = refs[:4], refs[4:8], refs[8], refs[9]
    which = pl.program_id(1)

    @pl.when((pl.program_id(0) == 0) & (which == 0))
    def _():
        _, core, zhi, y, x = (pos[i] for i in range(5))
        position = lax.broadcasted_iota(jnp.int32, (1, ROWS), 1)
        row = lax.broadcasted_iota(jnp.int32, (ROWS, ROWS), 0).astype(F32)
        for w in range(2):
            wanted = fragment_row(position, core if w == 0 else 1 - core, zhi, y, x)
            order[w] = jnp.where(row == wanted, 1.0, 0.0).astype(BF16)

    for w, parts in enumerate((mine, theirs)):

        @pl.when(which == w)
        def _():
            rows = jnp.concatenate([p[...] for p in parts], axis=0)
            out[...] = jnp.dot(order[w], rows, preferred_element_type=F32).astype(BF16)


def place(pos, mine, theirs):
    half = mine[0].shape[1]
    share = half // N_ZLO
    part = pl.BlockSpec((QUARTER, share), lambda k, w, p: (0, k))
    return pl.pallas_call(
        place_kernel,
        grid_spec=pltpu.PrefetchScalarGridSpec(
            num_scalar_prefetch=1,
            grid=(N_ZLO, 2),
            in_specs=[part] * 8,
            out_specs=pl.BlockSpec(
                (ROWS, share), lambda k, w, p: (0, 2 * k + jnp.where(w == 0, p[1], 1 - p[1]))
            ),
            scratch_shapes=[pltpu.VMEM((2, ROWS, ROWS), BF16)],
        ),
        out_shape=jax.ShapeDtypeStruct((ROWS, 2 * half), BF16),
        compiler_params=pltpu.CompilerParams(vmem_limit_bytes=32 * MIB),
        name="place",
    )(pos, *mine, *theirs)


def local(activations, upstream, drift, first_moment, second_moment, outer_base, outer_momentum, scale_exponents):
    island = lax.axis_index("island")
    fsdp = lax.axis_index("fsdp")
    pos = jnp.stack([island // 2, island % 2, fsdp // 16, (fsdp // RING) % RING, fsdp % RING]).astype(jnp.int32)
    width = outer_base.shape[1]

    chunks = product(pos, upstream, activations, 0, width, 512)
    arrived = [send(chunks[j], along_a(j)) for j in (2, 1, 3)]
    chunks = add_first([chunks[0], *arrived], 1024)
    arrived = [send(chunks[j], along_b(j)) for j in (2, 1, 3)]
    keep, away = add_second([chunks[0], *arrived])
    arrived = send(away, OTHER_ZHI)

    first_new, second_new, own, away, unscale = inner_step(
        pos, keep, arrived, drift, first_moment, second_moment, outer_base, scale_exponents
    )
    coded = add_cores(own, send(away, OTHER_CORE))
    parts = [coded] + [send(coded, other_zlo(k)) for k in (1, 2, 3)]
    momentum_out, base_out, piece = outer_step(pos, parts, unscale, outer_momentum, outer_base)

    piece = join_pair(piece, send(piece, OTHER_ZHI))
    piece = join_four([piece] + [send(piece, along_b(-j)) for j in (1, 2, 3)])
    mine = [piece] + [send(piece, along_a(-j)) for j in (1, 2, 3)]
    theirs = [send(m, OTHER_CORE) for m in mine]
    fragment = place(pos, mine, theirs)
    return (first_new, second_new, momentum_out, base_out, fragment)


def solution(mesh):
    in_specs = (
        P("island", "fsdp", None),
        P("island", "fsdp", None),
        P("island", "fsdp", None),
        P("island", "fsdp", None),
        P("island", "fsdp", None),
        P("fsdp", None),
        P("fsdp", None),
        P("fsdp", None),
    )
    out_specs = (
        P("island", "fsdp", None),
        P("island", "fsdp", None),
        P("fsdp", "island"),
        P("fsdp", "island"),
        P(),
    )
    return jax.shard_map(local, mesh=mesh, in_specs=in_specs, out_specs=out_specs, check_vma=False)
```

```python
import functools

import jax
import jax.numpy as jnp
import numpy as np
from jax import lax
from jax.experimental import pallas as pl
from jax.experimental.pallas import tpu as pltpu
from jax.sharding import PartitionSpec as P

INNER_RATE = 0.02
OUTER_RATE = 0.7
BETA_FIRST = 0.9
BETA_SECOND = 0.95
CORRECT_FIRST = 1.0 - 0.9**10
CORRECT_SECOND = 1.0 - 0.95**10
WEIGHT_DECAY = 0.1
EPSILON = 1e-08
NESTEROV_MU = 0.9

N_ISLAND = 8
N_FSDP = 32
N_ZLO = 4
RING = 4
OWN = 12
ROWS = 384
QUARTER = ROWS // 4
PAIR = 2 * OWN
BLOCK = 128
MIB = 1 << 20
BF16 = jnp.bfloat16
F32 = jnp.float32
TILE = 1280
AXES = ("island", "fsdp")
SCALARS = pl.BlockSpec(memory_space=pltpu.SMEM)
IN_VMEM = pl.BlockSpec(memory_space=pltpu.VMEM)
IN_HBM = pl.BlockSpec(memory_space=pltpu.HBM)
SMALL = pltpu.CompilerParams(vmem_limit_bytes=16 * MIB)


def device_pairs(target):
    pairs = []
    for zlo in range(N_ZLO):
        for core in range(2):
            for zhi in range(2):
                for y in range(RING):
                    for x in range(RING):
                        here = (zlo, core, zhi, y, x)
                        pairs.append((device_id(*here), device_id(*target(*here))))
    return pairs


def device_id(zlo, core, zhi, y, x):
    return (zlo * 2 + core) * N_FSDP + (zhi * RING + y) * RING + x


def along_a(step):
    def target(zlo, core, zhi, y, x):
        if core == 0:
            return (zlo, core, zhi, y, (x + step) % RING)
        return (zlo, core, zhi, (y + step) % RING, x)

    return device_pairs(target)


def along_b(step):
    def target(zlo, core, zhi, y, x):
        if core == 0:
            return (zlo, core, zhi, (y + step) % RING, x)
        return (zlo, core, zhi, y, (x + step) % RING)

    return device_pairs(target)


OTHER_ZHI = device_pairs(lambda zlo, core, zhi, y, x: (zlo, core, 1 - zhi, y, x))
NEAR_OTHER_ZHI = device_pairs(lambda zlo, core, zhi, y, x: (zlo ^ 2, core, 1 - zhi, y, x))
OTHER_CORE = device_pairs(lambda zlo, core, zhi, y, x: (zlo, 1 - core, zhi, y, x))


def other_zlo(k):
    return device_pairs(lambda zlo, core, zhi, y, x: (zlo ^ k, core, zhi, y, x))


def send(value, pairs):
    return lax.ppermute(value, AXES, pairs)


def coordinates(pos):
    device = pos[0]
    bit = lambda low, count: lax.bitwise_and(lax.shift_right_logical(device, jnp.int32(low)), jnp.int32(count - 1))
    return bit(6, N_ZLO), bit(5, 2), bit(4, 2), bit(2, RING), bit(0, RING)


def fragment_row(position, core, zhi, y, x):
    position = position.astype(F32)
    ja = jnp.floor((position + 0.5) / QUARTER)
    rest = position - QUARTER * ja
    jb = jnp.floor((rest + 0.5) / PAIR)
    rest = rest - PAIR * jb
    jz = jnp.floor((rest + 0.5) / OWN)
    r = rest - OWN * jz
    first = jnp.where(core == 0, ja, jb)
    second = jnp.where(core == 0, jb, ja)
    col = x.astype(F32) + first
    col = jnp.where(col >= RING, col - RING, col)
    line = y.astype(F32) + second
    line = jnp.where(line >= RING, line - RING, line)
    half = jnp.where(zhi == 0, jz, 1.0 - jz)
    return ((half * RING + line) * RING + col) * OWN + r


def order_kernel(pos, up_ref, *outs):
    _, core, zhi, y, x = coordinates(pos)
    wanted = fragment_row(lax.broadcasted_iota(jnp.int32, (ROWS, 1), 0), core, zhi, y, x)
    column = lax.broadcasted_iota(jnp.int32, (ROWS, ROWS), 1).astype(F32)
    pick = jnp.where(column == wanted, 1.0, 0.0).astype(BF16)
    up_rows = lax.dot_general(
        pick, up_ref[0], (((1,), (1,)), ((), ())), preferred_element_type=F32
    ).astype(BF16)
    outs[0][...] = up_rows[:QUARTER]
    outs[1][:QUARTER] = up_rows[QUARTER : 2 * QUARTER]
    outs[1][QUARTER:] = up_rows[3 * QUARTER :]
    outs[2][...] = up_rows[2 * QUARTER : 3 * QUARTER]


def order_rows(pos, upstream):
    tokens = upstream.shape[1]
    return pl.pallas_call(
        order_kernel,
        in_specs=[SCALARS, IN_VMEM],
        out_specs=[IN_VMEM] * 3,
        out_shape=[jax.ShapeDtypeStruct((n * QUARTER, tokens), BF16) for n in (1, 2, 1)],
        compiler_params=SMALL,
        name="order_rows",
    )(pos, upstream)


def product_kernel(up_rows, act_ref, *outs):
    width = act_ref.shape[2]
    chunks = up_rows.shape[0] // QUARTER
    pieces = len(outs) // chunks
    per_out = width // pieces
    for first in range(0, width, TILE):
        total = jnp.dot(
            up_rows[...], act_ref[0, :, first : first + TILE], preferred_element_type=F32
        ).astype(BF16)
        piece, place = divmod(first, per_out)
        for c in range(chunks):
            outs[c * pieces + piece][:, place : place + TILE] = total[c * QUARTER : (c + 1) * QUARTER]


def product(up_rows, activations, pieces):
    rows, tokens = up_rows.shape
    width = activations.shape[2]
    count = rows // QUARTER * pieces
    return pl.pallas_call(
        product_kernel,
        in_specs=[IN_VMEM, IN_VMEM],
        out_specs=[IN_VMEM] * count,
        out_shape=[jax.ShapeDtypeStruct((QUARTER, width // pieces), BF16)] * count,
        compiler_params=SMALL,
        cost_estimate=pl.CostEstimate(
            flops=2 * rows * tokens * width,
            bytes_accessed=2 * tokens * (width + rows) + 2 * rows * width,
            transcendentals=0,
        ),
        name="product",
    )(up_rows, activations)


def add_first_kernel(own, left_one, left_two, right_one, right_two, *outs):
    half = left_one.shape[1]
    for h, (one, two) in enumerate(((left_one, left_two), (right_one, right_two))):
        cols = slice(h * half, (h + 1) * half)
        total = own[:, cols].astype(F32) + (one[...].astype(F32) + two[...].astype(F32))
        for j in range(4):
            outs[j][:, cols] = total[j * PAIR : (j + 1) * PAIR].astype(BF16)


def add_first(parts):
    return pl.pallas_call(
        add_first_kernel,
        out_shape=[jax.ShapeDtypeStruct((PAIR, parts[0].shape[1]), BF16)] * 4,
        compiler_params=SMALL,
        name="add_first",
    )(*parts)


def packed(rows):
    half = rows.shape[1] // 2
    return jnp.concatenate([rows[:, :half], rows[:, half:]], axis=0).astype(BF16)


def add_second_kernel(own, one, two, three, keep, away):
    total = (own[...].astype(F32) + one[...].astype(F32)) + (
        two[...].astype(F32) + three[...].astype(F32)
    )
    keep[...] = total[:OWN]
    away[...] = packed(total[OWN:])


def add_second(parts):
    width = parts[0].shape[1]
    return pl.pallas_call(
        add_second_kernel,
        out_shape=[
            jax.ShapeDtypeStruct((OWN, width), F32),
            jax.ShapeDtypeStruct((PAIR, width // 2), BF16),
        ],
        compiler_params=SMALL,
        name="add_second",
    )(*parts)


def inner_kernel(pos, keep, arrived, drift, first, second, base, exponents, first_out, second_out, own, away, unscale_out):
    _, core, _, _, _ = coordinates(pos)
    width = keep.shape[1]
    share = width // N_ISLAND
    per_share = share // BLOCK
    exponent = exponents[...].astype(F32)
    scaling_all = jnp.exp2(-exponent)
    unscale_all = jnp.exp2(exponent)

    def spread(values, i):
        return jnp.concatenate(
            [
                jnp.broadcast_to(values[:, b : b + 1], (OWN, BLOCK))
                for b in range(i * per_share, (i + 1) * per_share)
            ],
            axis=1,
        )

    def coded_share(i, received):
        cols = slice(i * share, (i + 1) * share)
        gradient = keep[:, cols] + received
        base_now = base[:, cols]
        params = base_now + drift[0, :, cols]
        first_new = BETA_FIRST * first[0, :, cols] + (1.0 - BETA_FIRST) * gradient
        second_new = BETA_SECOND * second[0, :, cols] + (1.0 - BETA_SECOND) * gradient * gradient
        first_out[0, :, cols] = first_new
        second_out[0, :, cols] = second_new
        update = (
            first_new / CORRECT_FIRST / (jnp.sqrt(second_new / CORRECT_SECOND) + EPSILON)
            + WEIGHT_DECAY * params
        )
        inner = params - INNER_RATE * update
        return jnp.clip((base_now - inner) * spread(scaling_all, i), -127.0, 127.0)

    for i in range(N_ISLAND // 2):
        received = arrived[:, i * share : (i + 1) * share].astype(F32)
        upper = coded_share(i, received[:OWN])
        lower = coded_share(i + N_ISLAND // 2, received[OWN:])
        coded = jnp.concatenate([upper, lower], axis=0).astype(BF16)
        place = slice((i // 2) * share, (i // 2 + 1) * share)
        place_lower = slice((i // 2 + 2) * share, (i // 2 + 3) * share)

        @pl.when(core == i % 2)
        def _():
            own[:, place] = coded
            unscale_out[:, place] = spread(unscale_all, i)
            unscale_out[:, place_lower] = spread(unscale_all, i + N_ISLAND // 2)

        @pl.when(core != i % 2)
        def _():
            away[:, place] = coded


def inner_step(pos, keep, arrived, drift, first, second, base, exponents):
    width = keep.shape[1]
    return pl.pallas_call(
        inner_kernel,
        in_specs=[SCALARS] + [IN_VMEM] * 7,
        out_specs=[IN_VMEM] * 5,
        out_shape=[
            jax.ShapeDtypeStruct(first.shape, F32),
            jax.ShapeDtypeStruct(second.shape, F32),
            jax.ShapeDtypeStruct((PAIR, width // 4), BF16),
            jax.ShapeDtypeStruct((PAIR, width // 4), BF16),
            jax.ShapeDtypeStruct((OWN, width // 2), F32),
        ],
        compiler_params=SMALL,
        name="inner_step",
    )(pos, keep, arrived, drift, first, second, base, exponents)


def add_two_kernel(own, arrived, out):
    out[...] = (own[...].astype(F32) + arrived[...].astype(F32)).astype(BF16)


def add_two(own, arrived):
    return pl.pallas_call(
        add_two_kernel,
        out_shape=jax.ShapeDtypeStruct(own.shape, BF16),
        compiler_params=SMALL,
        name="add_two",
    )(own, arrived)


def outer_kernel(pos, own, one, two, three, unscale, momentum, base, momentum_out, base_out, fragment):
    zlo, core, _, _, _ = coordinates(pos)
    share = own.shape[1] // 2

    def outer_share(k, summed):
        cols = pl.ds(pl.multiple_of((2 * k + core) * share, BLOCK), share)
        pseudo = summed * unscale[:, k * share : (k + 1) * share] / N_ISLAND
        momentum_next = NESTEROV_MU * momentum[:, cols] + pseudo
        base_next = base[:, cols] - OUTER_RATE * (pseudo + NESTEROV_MU * momentum_next)

        @pl.when(zlo == k)
        def _():
            momentum_out[...] = momentum_next
            base_out[...] = base_next

        return base_next

    for k in range(N_ZLO // 2):
        place = slice(k * share, (k + 1) * share)
        summed = (own[:, place].astype(F32) + one[:, place].astype(F32)) + (
            two[:, place].astype(F32) + three[:, place].astype(F32)
        )
        upper = outer_share(k, summed[:OWN])
        lower = outer_share(k + 2, summed[OWN:])
        fragment[:, place] = jnp.concatenate([upper, lower], axis=0).astype(BF16)


def outer_step(pos, parts, unscale, momentum, base):
    width = base.shape[1]
    return pl.pallas_call(
        outer_kernel,
        in_specs=[SCALARS] + [IN_VMEM] * 7,
        out_specs=[IN_VMEM] * 3,
        out_shape=[
            jax.ShapeDtypeStruct((OWN, width // N_ISLAND), F32),
            jax.ShapeDtypeStruct((OWN, width // N_ISLAND), F32),
            jax.ShapeDtypeStruct((PAIR, width // 4), BF16),
        ],
        compiler_params=SMALL,
        name="outer_step",
    )(pos, *parts, unscale, momentum, base)


def join_kernel(*refs):
    *parts, out = refs
    out[...] = jnp.concatenate([p[...].astype(F32) for p in parts], axis=0).astype(BF16)


def join(parts):
    rows, width = parts[0].shape
    return pl.pallas_call(
        join_kernel,
        out_shape=jax.ShapeDtypeStruct((len(parts) * rows, width), BF16),
        compiler_params=SMALL,
        name="join",
    )(*parts)


def place_kernel(w, pos, *refs):
    parts = refs[:4]
    out, held, sent = refs[-3:]
    _, core, zhi, y, x = coordinates(pos)
    whose = core if w == 0 else 1 - core
    line_rows = RING * OWN
    share = parts[0].shape[1] // 2

    def fill(a_is_x, x_here, k, b):
        source = pl.ds(pl.multiple_of(k * share + b * BLOCK, BLOCK), BLOCK)
        rows = [p[:, source].astype(F32) for p in parts]
        for jz in range(2):
            half = zhi if jz == 0 else 1 - zhi
            for h in range(2):
                target = pl.ds(pl.multiple_of((2 * h + k) * share + b * BLOCK, BLOCK), BLOCK)
                for q in range(RING):
                    pieces = []
                    for x_there in range(RING):
                        jx = (x_there - x_here) % RING
                        ja, jb = (jx, q) if a_is_x else (q, jx)
                        first = (jb * 2 + jz) * PAIR + h * OWN
                        pieces.append(rows[ja][first : first + OWN])
                    line = half * RING + lax.rem(y + q, RING)
                    start = pl.multiple_of(line * line_rows, 16)
                    held[pl.ds(start, line_rows), target] = jnp.concatenate(pieces, axis=0).astype(BF16)

    copies = []
    for k in range(2):
        for a_is_x in (True, False):
            for x_here in range(RING):

                @pl.when(((whose == 0) == a_is_x) & (x == x_here))
                def _():
                    @pl.loop(0, share // BLOCK)
                    def _(b):
                        fill(a_is_x, x_here, k, b)

        for zlo in (k, 2 + k):
            cols = pl.ds(pl.multiple_of((2 * zlo + whose) * share, BLOCK), share)
            copies.append(
                pltpu.make_async_copy(
                    held.at[:, pl.ds(zlo * share, share)], out.at[:, cols], sent.at[len(copies)]
                )
            )
            copies[-1].start()
    for copy in copies:
        copy.wait()


def place(w, pos, parts, fragment=None):
    width = 4 * parts[0].shape[1]
    again = () if fragment is None else (fragment,)
    return pl.pallas_call(
        functools.partial(place_kernel, w),
        in_specs=[SCALARS] + [IN_VMEM] * 4 + [IN_HBM] * len(again),
        out_specs=IN_HBM,
        out_shape=jax.ShapeDtypeStruct((ROWS, width), BF16),
        scratch_shapes=[pltpu.VMEM((ROWS, width // 2), BF16), pltpu.SemaphoreType.DMA((4,))],
        input_output_aliases={5: 0} if again else {},
        compiler_params=SMALL,
        name="place",
    )(pos, *parts, *again)


def local(activations, upstream, drift, first_moment, second_moment, outer_base, outer_momentum, scale_exponents):
    pos = lax.axis_index(AXES).astype(jnp.int32).reshape(1)

    up_own, up_sides, up_far = order_rows(pos, upstream)
    far_left, far_right = product(up_far, activations, 2)
    via_left = send(far_left, along_a(1))
    via_right = send(far_right, along_a(-1))
    next_left, next_right, last_left, last_right = product(up_sides, activations, 2)
    right_one = send(next_right, along_a(1))
    left_two = send(last_left, along_a(-1))
    (own,) = product(up_own, activations, 1)
    left_one = send(add_two(next_left, via_left), along_a(1))
    right_two = send(add_two(last_right, via_right), along_a(-1))
    chunks = add_first([own, left_one, left_two, right_one, right_two])
    keep, away = add_second([chunks[0]] + [send(chunks[j], along_b(j)) for j in (2, 1, 3)])
    arrived = send(away, OTHER_ZHI)

    first_new, second_new, own, away, unscale = inner_step(
        pos, keep, arrived, drift, first_moment, second_moment, outer_base, scale_exponents
    )
    coded = add_two(own, send(away, OTHER_CORE))
    parts = [send(coded, other_zlo(k)) for k in (1, 2, 3)]
    flat = (first_new.size // BLOCK, BLOCK)
    first_flat, second_flat, *parts = lax.optimization_barrier(
        (first_new.reshape(flat), second_new.reshape(flat), *parts)
    )
    momentum_out, base_out, piece = outer_step(pos, [coded, *parts], unscale, outer_momentum, outer_base)

    piece = join([piece, send(piece, NEAR_OTHER_ZHI)])
    line = {j: send(piece, along_b(-j)) for j in (2, 1, 3)}
    piece = join([piece, line[1], line[2], line[3]])
    plane = {j: send(piece, along_a(-j)) for j in (2, 1, 3)}
    mine = [piece, plane[1], plane[2], plane[3]]
    theirs = [send(m, OTHER_CORE) for m in mine]
    fragment = place(1, pos, theirs, place(0, pos, mine))
    return (
        first_flat.reshape(first_new.shape),
        second_flat.reshape(second_new.shape),
        momentum_out,
        base_out,
        fragment,
    )


def solution(mesh):
    in_specs = (
        P("island", "fsdp", None),
        P("island", "fsdp", None),
        P("island", "fsdp", None),
        P("island", "fsdp", None),
        P("island", "fsdp", None),
        P("fsdp", None),
        P("fsdp", None),
        P("fsdp", None),
    )
    out_specs = (
        P("island", "fsdp", None),
        P("island", "fsdp", None),
        P("fsdp", "island"),
        P("fsdp", "island"),
        P(),
    )
    return jax.shard_map(local, mesh=mesh, in_specs=in_specs, out_specs=out_specs, check_vma=False)
```

```python
import functools

import jax
import jax.numpy as jnp
import numpy as np
from jax import lax
from jax.experimental import pallas as pl
from jax.experimental.pallas import tpu as pltpu
from jax.sharding import PartitionSpec as P

INNER_RATE = 0.02
OUTER_RATE = 0.7
BETA_FIRST = 0.9
BETA_SECOND = 0.95
CORRECT_FIRST = 1.0 - 0.9**10
CORRECT_SECOND = 1.0 - 0.95**10
WEIGHT_DECAY = 0.1
EPSILON = 1e-08
NESTEROV_MU = 0.9

N_ISLAND = 8
N_FSDP = 32
N_ZLO = 4
RING = 4
OWN = 12
ROWS = 384
QUARTER = ROWS // 4
PAIR = 2 * OWN
BLOCK = 128
MIB = 1 << 20
BF16 = jnp.bfloat16
F32 = jnp.float32
TILE = 1280
READ_TILE = 1280
AHEAD = 2
AXES = ("island", "fsdp")
SCALARS = pl.BlockSpec(memory_space=pltpu.SMEM)
IN_VMEM = pl.BlockSpec(memory_space=pltpu.VMEM)
IN_HBM = pl.BlockSpec(memory_space=pltpu.HBM)
SMALL = pltpu.CompilerParams(vmem_limit_bytes=16 * MIB)


def device_pairs(target):
    pairs = []
    for zlo in range(N_ZLO):
        for core in range(2):
            for zhi in range(2):
                for y in range(RING):
                    for x in range(RING):
                        here = (zlo, core, zhi, y, x)
                        pairs.append((device_id(*here), device_id(*target(*here))))
    return pairs


def device_id(zlo, core, zhi, y, x):
    return (zlo * 2 + core) * N_FSDP + (zhi * RING + y) * RING + x


def along_a(step):
    def target(zlo, core, zhi, y, x):
        if core == 0:
            return (zlo, core, zhi, y, (x - step) % RING)
        return (zlo, core, zhi, (y - step) % RING, x)

    return device_pairs(target)


def along_b(step):
    def target(zlo, core, zhi, y, x):
        if core == 0:
            return (zlo, core, zhi, (y - step) % RING, x)
        return (zlo, core, zhi, y, (x - step) % RING)

    return device_pairs(target)


OTHER_ZHI = device_pairs(lambda zlo, core, zhi, y, x: (zlo, core, 1 - zhi, y, x))
NEAR_OTHER_ZHI = device_pairs(lambda zlo, core, zhi, y, x: (zlo ^ 2, core, 1 - zhi, y, x))
OTHER_CORE = device_pairs(lambda zlo, core, zhi, y, x: (zlo, 1 - core, zhi, y, x))


def other_zlo(k):
    return device_pairs(lambda zlo, core, zhi, y, x: (zlo ^ k, core, zhi, y, x))


def send(value, pairs):
    return lax.ppermute(value, AXES, pairs)


def coordinates(pos):
    device = pos[0]
    bit = lambda low, count: lax.bitwise_and(lax.shift_right_logical(device, jnp.int32(low)), jnp.int32(count - 1))
    return bit(6, N_ZLO), bit(5, 2), bit(4, 2), bit(2, RING), bit(0, RING)


def fragment_row(position, core, zhi, y, x):
    position = position.astype(F32)
    ja = jnp.floor((position + 0.5) / QUARTER)
    rest = position - QUARTER * ja
    jb = jnp.floor((rest + 0.5) / PAIR)
    rest = rest - PAIR * jb
    jz = jnp.floor((rest + 0.5) / OWN)
    r = rest - OWN * jz
    first = jnp.where(core == 0, ja, jb)
    second = jnp.where(core == 0, jb, ja)
    col = x.astype(F32) - first
    col = jnp.where(col < 0, col + RING, col)
    line = y.astype(F32) - second
    line = jnp.where(line < 0, line + RING, line)
    half = jnp.where(zhi == 0, jz, 1.0 - jz)
    return ((half * RING + line) * RING + col) * OWN + r


def far_kernel(pos, up_ref, act_ref, left, right, up_sides, up_own, act_held, up_held, up_arrived, arrived):
    up_copy = pltpu.make_async_copy(up_ref.at[0], up_held, up_arrived)
    up_copy.start()
    tiles = act_ref.shape[2] // READ_TILE
    copies = []
    for t in range(tiles):
        cols = pl.ds(t * READ_TILE, READ_TILE)
        copies.append(
            pltpu.make_async_copy(act_ref.at[0, :, cols], act_held.at[0, :, cols], arrived.at[t])
        )
    for copy in copies[:AHEAD]:
        copy.start()
    _, core, zhi, y, x = coordinates(pos)
    wanted = fragment_row(lax.broadcasted_iota(jnp.int32, (ROWS, 1), 0), core, zhi, y, x)
    column = lax.broadcasted_iota(jnp.int32, (ROWS, ROWS), 1).astype(F32)
    pick = jnp.where(column == wanted, 1.0, 0.0).astype(BF16)
    up_copy.wait()
    up_rows = lax.dot_general(
        pick, up_held[...], (((1,), (1,)), ((), ())), preferred_element_type=F32
    ).astype(BF16)
    up_own[...] = up_rows[:QUARTER]
    up_sides[:QUARTER] = up_rows[QUARTER : 2 * QUARTER]
    up_sides[QUARTER:] = up_rows[3 * QUARTER :]
    up_far = up_rows[2 * QUARTER : 3 * QUARTER]
    half = left.shape[1]
    for t in range(tiles):
        copies[t].wait()
        if t + AHEAD < tiles:
            copies[t + AHEAD].start()
        first = t * READ_TILE
        out, place = (left, first) if first < half else (right, first - half)
        out[:, place : place + READ_TILE] = jnp.dot(
            up_far, act_held[0, :, first : first + READ_TILE], preferred_element_type=F32
        ).astype(BF16)


def far_product(pos, upstream, activations):
    _, tokens, width = activations.shape
    shapes = [
        (QUARTER, width // 2),
        (QUARTER, width // 2),
        (2 * QUARTER, tokens),
        (QUARTER, tokens),
        activations.shape,
    ]
    return pl.pallas_call(
        far_kernel,
        in_specs=[SCALARS, IN_HBM, IN_HBM],
        out_specs=[IN_VMEM] * 5,
        out_shape=[jax.ShapeDtypeStruct(shape, BF16) for shape in shapes],
        scratch_shapes=[
            pltpu.VMEM((tokens, ROWS), BF16),
            pltpu.SemaphoreType.DMA,
            pltpu.SemaphoreType.DMA((width // READ_TILE,)),
        ],
        compiler_params=SMALL,
        name="far_product",
    )(
        pos,
        pltpu.with_memory_space_constraint(upstream, pltpu.HBM),
        pltpu.with_memory_space_constraint(activations, pltpu.HBM),
    )


def product_kernel(up_rows, act_ref, *outs):
    width = act_ref.shape[2]
    chunks = up_rows.shape[0] // QUARTER
    pieces = len(outs) // chunks
    per_out = width // pieces
    for first in range(0, width, TILE):
        total = jnp.dot(
            up_rows[...], act_ref[0, :, first : first + TILE], preferred_element_type=F32
        ).astype(BF16)
        piece, place = divmod(first, per_out)
        for c in range(chunks):
            outs[c * pieces + piece][:, place : place + TILE] = total[c * QUARTER : (c + 1) * QUARTER]


def product(up_rows, activations, pieces):
    rows, tokens = up_rows.shape
    width = activations.shape[2]
    count = rows // QUARTER * pieces
    return pl.pallas_call(
        product_kernel,
        in_specs=[IN_VMEM, IN_VMEM],
        out_specs=[IN_VMEM] * count,
        out_shape=[jax.ShapeDtypeStruct((QUARTER, width // pieces), BF16)] * count,
        compiler_params=SMALL,
        cost_estimate=pl.CostEstimate(
            flops=2 * rows * tokens * width,
            bytes_accessed=2 * tokens * (width + rows) + 2 * rows * width,
            transcendentals=0,
        ),
        name="product",
    )(up_rows, activations)


def add_first_kernel(own, left_one, left_two, right_one, right_two, *outs):
    half = left_one.shape[1]
    for h, (one, two) in enumerate(((left_one, left_two), (right_one, right_two))):
        cols = slice(h * half, (h + 1) * half)
        total = own[:, cols].astype(F32) + (one[...].astype(F32) + two[...].astype(F32))
        for j in range(4):
            outs[j][:, cols] = total[j * PAIR : (j + 1) * PAIR].astype(BF16)


def add_first(parts):
    return pl.pallas_call(
        add_first_kernel,
        out_shape=[jax.ShapeDtypeStruct((PAIR, parts[0].shape[1]), BF16)] * 4,
        compiler_params=SMALL,
        name="add_first",
    )(*parts)


def packed(rows):
    half = rows.shape[1] // 2
    return jnp.concatenate([rows[:, :half], rows[:, half:]], axis=0).astype(BF16)


def add_second_kernel(own, one, two, three, keep, away):
    total = (own[...].astype(F32) + one[...].astype(F32)) + (
        two[...].astype(F32) + three[...].astype(F32)
    )
    keep[...] = total[:OWN]
    away[...] = packed(total[OWN:])


def add_second(parts):
    width = parts[0].shape[1]
    return pl.pallas_call(
        add_second_kernel,
        out_shape=[
            jax.ShapeDtypeStruct((OWN, width), F32),
            jax.ShapeDtypeStruct((PAIR, width // 2), BF16),
        ],
        compiler_params=SMALL,
        name="add_second",
    )(*parts)


def inner_kernel(pos, keep, arrived, drift, first, second, base, exponents, first_out, second_out, own, away, unscale_out):
    _, core, _, _, _ = coordinates(pos)
    width = keep.shape[1]
    share = width // N_ISLAND
    per_share = share // BLOCK
    exponent = exponents[...].astype(F32)
    scaling_all = jnp.exp2(-exponent)
    unscale_all = jnp.exp2(exponent)

    def spread(values, i):
        return jnp.concatenate(
            [
                jnp.broadcast_to(values[:, b : b + 1], (OWN, BLOCK))
                for b in range(i * per_share, (i + 1) * per_share)
            ],
            axis=1,
        )

    def coded_share(i, received):
        cols = slice(i * share, (i + 1) * share)
        gradient = keep[:, cols] + received
        base_now = base[:, cols]
        params = base_now + drift[0, :, cols]
        first_new = BETA_FIRST * first[0, :, cols] + (1.0 - BETA_FIRST) * gradient
        second_new = BETA_SECOND * second[0, :, cols] + (1.0 - BETA_SECOND) * gradient * gradient
        first_out[0, :, cols] = first_new
        second_out[0, :, cols] = second_new
        update = (
            first_new / CORRECT_FIRST / (jnp.sqrt(second_new / CORRECT_SECOND) + EPSILON)
            + WEIGHT_DECAY * params
        )
        inner = params - INNER_RATE * update
        return jnp.clip((base_now - inner) * spread(scaling_all, i), -127.0, 127.0)

    for i in range(N_ISLAND // 2):
        received = arrived[:, i * share : (i + 1) * share].astype(F32)
        upper = coded_share(i, received[:OWN])
        lower = coded_share(i + N_ISLAND // 2, received[OWN:])
        coded = jnp.concatenate([upper, lower], axis=0).astype(BF16)
        place = slice((i // 2) * share, (i // 2 + 1) * share)
        place_lower = slice((i // 2 + 2) * share, (i // 2 + 3) * share)

        @pl.when(core == i % 2)
        def _():
            own[:, place] = coded
            unscale_out[:, place] = spread(unscale_all, i)
            unscale_out[:, place_lower] = spread(unscale_all, i + N_ISLAND // 2)

        @pl.when(core != i % 2)
        def _():
            away[:, place] = coded


def inner_step(pos, keep, arrived, drift, first, second, base, exponents):
    width = keep.shape[1]
    return pl.pallas_call(
        inner_kernel,
        in_specs=[SCALARS] + [IN_VMEM] * 7,
        out_specs=[IN_VMEM] * 5,
        out_shape=[
            jax.ShapeDtypeStruct(first.shape, F32),
            jax.ShapeDtypeStruct(second.shape, F32),
            jax.ShapeDtypeStruct((PAIR, width // 4), BF16),
            jax.ShapeDtypeStruct((PAIR, width // 4), BF16),
            jax.ShapeDtypeStruct((OWN, width // 2), F32),
        ],
        compiler_params=SMALL,
        name="inner_step",
    )(pos, keep, arrived, drift, first, second, base, exponents)


def add_two_kernel(own, arrived, out):
    out[...] = (own[...].astype(F32) + arrived[...].astype(F32)).astype(BF16)


def add_two(own, arrived):
    return pl.pallas_call(
        add_two_kernel,
        out_shape=jax.ShapeDtypeStruct(own.shape, BF16),
        compiler_params=SMALL,
        name="add_two",
    )(own, arrived)


def outer_kernel(pos, own, one, two, three, unscale, momentum, base, momentum_out, base_out, fragment):
    zlo, core, _, _, _ = coordinates(pos)
    share = own.shape[1] // 2

    def outer_share(k, summed):
        cols = pl.ds(pl.multiple_of((2 * k + core) * share, BLOCK), share)
        pseudo = summed * unscale[:, k * share : (k + 1) * share] / N_ISLAND
        momentum_next = NESTEROV_MU * momentum[:, cols] + pseudo
        base_next = base[:, cols] - OUTER_RATE * (pseudo + NESTEROV_MU * momentum_next)

        @pl.when(zlo == k)
        def _():
            momentum_out[...] = momentum_next
            base_out[...] = base_next

        return base_next

    for k in range(N_ZLO // 2):
        place = slice(k * share, (k + 1) * share)
        summed = (own[:, place].astype(F32) + one[:, place].astype(F32)) + (
            two[:, place].astype(F32) + three[:, place].astype(F32)
        )
        upper = outer_share(k, summed[:OWN])
        lower = outer_share(k + 2, summed[OWN:])
        fragment[:, place] = jnp.concatenate([upper, lower], axis=0).astype(BF16)


def outer_step(pos, parts, unscale, momentum, base):
    width = base.shape[1]
    return pl.pallas_call(
        outer_kernel,
        in_specs=[SCALARS] + [IN_VMEM] * 7,
        out_specs=[IN_VMEM] * 3,
        out_shape=[
            jax.ShapeDtypeStruct((OWN, width // N_ISLAND), F32),
            jax.ShapeDtypeStruct((OWN, width // N_ISLAND), F32),
            jax.ShapeDtypeStruct((PAIR, width // 4), BF16),
        ],
        compiler_params=SMALL,
        name="outer_step",
    )(pos, *parts, unscale, momentum, base)


def join_kernel(*refs):
    *parts, out = refs
    out[...] = jnp.concatenate([p[...].astype(F32) for p in parts], axis=0).astype(BF16)


def join(parts):
    rows, width = parts[0].shape
    return pl.pallas_call(
        join_kernel,
        out_shape=jax.ShapeDtypeStruct((len(parts) * rows, width), BF16),
        compiler_params=SMALL,
        name="join",
    )(*parts)


def place_kernel(w, pos, *refs):
    parts = refs[:4]
    out, held, sent = refs[-3:]
    _, core, zhi, y, x = coordinates(pos)
    whose = core if w == 0 else 1 - core
    line_rows = RING * OWN
    share = parts[0].shape[1] // 2

    def fill(a_is_x, x_here, k, b):
        source = pl.ds(pl.multiple_of(k * share + b * BLOCK, BLOCK), BLOCK)
        for q in range(RING):
            rows = []
            for x_there in range(RING):
                jx = (x_here - x_there) % RING
                ja, jb = (jx, q) if a_is_x else (q, jx)
                rows.append(parts[ja][jb * 2 * PAIR : (jb + 1) * 2 * PAIR, source].astype(F32))
            for jz in range(2):
                half = zhi if jz == 0 else 1 - zhi
                line = half * RING + lax.rem(y + RING - q, RING)
                start = pl.multiple_of(line * line_rows, 16)
                for h in range(2):
                    first = jz * PAIR + h * OWN
                    target = pl.ds(pl.multiple_of((2 * h + k) * share + b * BLOCK, BLOCK), BLOCK)
                    held[pl.ds(start, line_rows), target] = jnp.concatenate(
                        [r[first : first + OWN] for r in rows], axis=0
                    ).astype(BF16)

    copies = []
    for k in range(2):
        for a_is_x in (True, False):
            for x_here in range(RING):

                @pl.when(((whose == 0) == a_is_x) & (x == x_here))
                def _():
                    @pl.loop(0, share // BLOCK)
                    def _(b):
                        fill(a_is_x, x_here, k, b)

        for zlo in (k, 2 + k):
            cols = pl.ds(pl.multiple_of((2 * zlo + whose) * share, BLOCK), share)
            copies.append(
                pltpu.make_async_copy(
                    held.at[:, pl.ds(zlo * share, share)], out.at[:, cols], sent.at[len(copies)]
                )
            )
            copies[-1].start()
    for copy in copies:
        copy.wait()


def place(w, pos, parts, fragment=None):
    width = 4 * parts[0].shape[1]
    again = () if fragment is None else (fragment,)
    return pl.pallas_call(
        functools.partial(place_kernel, w),
        in_specs=[SCALARS] + [IN_VMEM] * 4 + [IN_HBM] * len(again),
        out_specs=IN_HBM,
        out_shape=jax.ShapeDtypeStruct((ROWS, width), BF16),
        scratch_shapes=[pltpu.VMEM((ROWS, width // 2), BF16), pltpu.SemaphoreType.DMA((4,))],
        input_output_aliases={5: 0} if again else {},
        compiler_params=SMALL,
        name="place",
    )(pos, *parts, *again)


def local(activations, upstream, drift, first_moment, second_moment, outer_base, outer_momentum, scale_exponents):
    pos = lax.axis_index(AXES).astype(jnp.int32).reshape(1)

    far_left, far_right, up_sides, up_own, activations = far_product(pos, upstream, activations)
    via_left = send(far_left, along_a(1))
    via_right = send(far_right, along_a(-1))
    next_left, next_right, last_left, last_right = product(up_sides, activations, 2)
    right_one = send(next_right, along_a(1))
    left_two = send(last_left, along_a(-1))
    (own,) = product(up_own, activations, 1)
    left_one = send(add_two(next_left, via_left), along_a(1))
    right_two = send(add_two(last_right, via_right), along_a(-1))
    chunks = add_first([own, left_one, left_two, right_one, right_two])
    keep, away = add_second([chunks[0]] + [send(chunks[j], along_b(j)) for j in (2, 1, 3)])
    arrived = send(away, OTHER_ZHI)

    first_new, second_new, own, away, unscale = inner_step(
        pos, keep, arrived, drift, first_moment, second_moment, outer_base, scale_exponents
    )
    coded = add_two(own, send(away, OTHER_CORE))
    parts = [send(coded, other_zlo(k)) for k in (1, 2, 3)]
    flat = (first_new.size // BLOCK, BLOCK)
    first_flat, second_flat, *parts = lax.optimization_barrier(
        (first_new.reshape(flat), second_new.reshape(flat), *parts)
    )
    momentum_out, base_out, piece = outer_step(pos, [coded, *parts], unscale, outer_momentum, outer_base)

    piece = join([piece, send(piece, NEAR_OTHER_ZHI)])
    line = {j: send(piece, along_b(-j)) for j in (2, 1, 3)}
    piece = join([piece, line[1], line[2], line[3]])
    plane = {j: send(piece, along_a(-j)) for j in (2, 1, 3)}
    mine = [piece, plane[1], plane[2], plane[3]]
    theirs = [send(m, OTHER_CORE) for m in mine]
    fragment = place(1, pos, theirs, place(0, pos, mine))
    return (
        first_flat.reshape(first_new.shape),
        second_flat.reshape(second_new.shape),
        momentum_out,
        base_out,
        fragment,
    )


def solution(mesh):
    in_specs = (
        P("island", "fsdp", None),
        P("island", "fsdp", None),
        P("island", "fsdp", None),
        P("island", "fsdp", None),
        P("island", "fsdp", None),
        P("fsdp", None),
        P("fsdp", None),
        P("fsdp", None),
    )
    out_specs = (
        P("island", "fsdp", None),
        P("island", "fsdp", None),
        P("fsdp", "island"),
        P("fsdp", "island"),
        P(),
    )
    return jax.shard_map(local, mesh=mesh, in_specs=in_specs, out_specs=out_specs, check_vma=False)
```

```python
import functools

import jax
import jax.numpy as jnp
import numpy as np
from jax import lax
from jax.experimental import pallas as pl
from jax.experimental.pallas import tpu as pltpu
from jax.sharding import PartitionSpec as P

INNER_RATE = 0.02
OUTER_RATE = 0.7
BETA_FIRST = 0.9
BETA_SECOND = 0.95
CORRECT_FIRST = 1.0 - 0.9**10
CORRECT_SECOND = 1.0 - 0.95**10
WEIGHT_DECAY = 0.1
EPSILON = 1e-08
NESTEROV_MU = 0.9

N_ISLAND = 8
N_FSDP = 32
N_ZLO = 4
RING = 4
OWN = 12
ROWS = 384
QUARTER = ROWS // 4
PAIR = 2 * OWN
BLOCK = 128
MIB = 1 << 20
BF16 = jnp.bfloat16
F32 = jnp.float32
TILE = 1280
READ_TILE = 2560
AHEAD = 2
AXES = ("island", "fsdp")
SCALARS = pl.BlockSpec(memory_space=pltpu.SMEM)
IN_VMEM = pl.BlockSpec(memory_space=pltpu.VMEM)
IN_HBM = pl.BlockSpec(memory_space=pltpu.HBM)
SMALL = pltpu.CompilerParams(vmem_limit_bytes=16 * MIB)


def device_pairs(target):
    pairs = []
    for zlo in range(N_ZLO):
        for core in range(2):
            for zhi in range(2):
                for y in range(RING):
                    for x in range(RING):
                        here = (zlo, core, zhi, y, x)
                        pairs.append((device_id(*here), device_id(*target(*here))))
    return pairs


def device_id(zlo, core, zhi, y, x):
    return (zlo * 2 + core) * N_FSDP + (zhi * RING + y) * RING + x


def along_a(step):
    def target(zlo, core, zhi, y, x):
        if core == 0:
            return (zlo, core, zhi, y, (x - step) % RING)
        return (zlo, core, zhi, (y - step) % RING, x)

    return device_pairs(target)


def along_b(step):
    def target(zlo, core, zhi, y, x):
        if core == 0:
            return (zlo, core, zhi, (y - step) % RING, x)
        return (zlo, core, zhi, y, (x - step) % RING)

    return device_pairs(target)


OTHER_ZHI = device_pairs(lambda zlo, core, zhi, y, x: (zlo, core, 1 - zhi, y, x))
NEAR_OTHER_ZHI = device_pairs(lambda zlo, core, zhi, y, x: (zlo ^ 2, core, 1 - zhi, y, x))
OTHER_CORE = device_pairs(lambda zlo, core, zhi, y, x: (zlo, 1 - core, zhi, y, x))


def other_zlo(k):
    return device_pairs(lambda zlo, core, zhi, y, x: (zlo ^ k, core, zhi, y, x))


def send(value, pairs):
    return lax.ppermute(value, AXES, pairs)


def coordinates(pos):
    device = pos[0]
    bit = lambda low, count: lax.bitwise_and(lax.shift_right_logical(device, jnp.int32(low)), jnp.int32(count - 1))
    return bit(6, N_ZLO), bit(5, 2), bit(4, 2), bit(2, RING), bit(0, RING)


def fragment_row(position, core, zhi, y, x):
    position = position.astype(F32)
    ja = jnp.floor((position + 0.5) / QUARTER)
    rest = position - QUARTER * ja
    jb = jnp.floor((rest + 0.5) / PAIR)
    rest = rest - PAIR * jb
    jz = jnp.floor((rest + 0.5) / OWN)
    r = rest - OWN * jz
    first = jnp.where(core == 0, ja, jb)
    second = jnp.where(core == 0, jb, ja)
    col = x.astype(F32) - first
    col = jnp.where(col < 0, col + RING, col)
    line = y.astype(F32) - second
    line = jnp.where(line < 0, line + RING, line)
    half = jnp.where(zhi == 0, jz, 1.0 - jz)
    return ((half * RING + line) * RING + col) * OWN + r


def far_kernel(pos, up_ref, act_ref, left, right, up_sides, up_own, act_held, up_held, up_arrived, arrived):
    up_copy = pltpu.make_async_copy(up_ref.at[0], up_held, up_arrived)
    up_copy.start()
    tiles = act_ref.shape[2] // READ_TILE
    copies = []
    for t in range(tiles):
        cols = pl.ds(t * READ_TILE, READ_TILE)
        copies.append(
            pltpu.make_async_copy(act_ref.at[0, :, cols], act_held.at[0, :, cols], arrived.at[t])
        )
    for copy in copies[:AHEAD]:
        copy.start()
    _, core, zhi, y, x = coordinates(pos)
    wanted = fragment_row(lax.broadcasted_iota(jnp.int32, (ROWS, 1), 0), core, zhi, y, x)
    column = lax.broadcasted_iota(jnp.int32, (ROWS, ROWS), 1).astype(F32)
    pick = jnp.where(column == wanted, 1.0, 0.0).astype(BF16)
    up_copy.wait()
    up_rows = lax.dot_general(
        pick, up_held[...], (((1,), (1,)), ((), ())), preferred_element_type=F32
    ).astype(BF16)
    up_own[...] = up_rows[:QUARTER]
    up_sides[:QUARTER] = up_rows[QUARTER : 2 * QUARTER]
    up_sides[QUARTER:] = up_rows[3 * QUARTER :]
    up_far = up_rows[2 * QUARTER : 3 * QUARTER]
    half = left.shape[1]
    for t in range(tiles):
        copies[t].wait()
        if t + AHEAD < tiles:
            copies[t + AHEAD].start()
        first = t * READ_TILE
        out, place = (left, first) if first < half else (right, first - half)
        out[:, place : place + READ_TILE] = jnp.dot(
            up_far, act_held[0, :, first : first + READ_TILE], preferred_element_type=F32
        ).astype(BF16)


def far_product(pos, upstream, activations):
    _, tokens, width = activations.shape
    shapes = [
        (QUARTER, width // 2),
        (QUARTER, width // 2),
        (2 * QUARTER, tokens),
        (QUARTER, tokens),
        activations.shape,
    ]
    return pl.pallas_call(
        far_kernel,
        in_specs=[SCALARS, IN_HBM, IN_HBM],
        out_specs=[IN_VMEM] * 5,
        out_shape=[jax.ShapeDtypeStruct(shape, BF16) for shape in shapes],
        scratch_shapes=[
            pltpu.VMEM((tokens, ROWS), BF16),
            pltpu.SemaphoreType.DMA,
            pltpu.SemaphoreType.DMA((width // READ_TILE,)),
        ],
        compiler_params=SMALL,
        name="far_product",
    )(
        pos,
        pltpu.with_memory_space_constraint(upstream, pltpu.HBM),
        pltpu.with_memory_space_constraint(activations, pltpu.HBM),
    )


def product_kernel(up_rows, act_ref, *outs):
    width = act_ref.shape[2]
    chunks = up_rows.shape[0] // QUARTER
    pieces = len(outs) // chunks
    per_out = width // pieces
    for first in range(0, width, TILE):
        total = jnp.dot(
            up_rows[...], act_ref[0, :, first : first + TILE], preferred_element_type=F32
        ).astype(BF16)
        piece, place = divmod(first, per_out)
        for c in range(chunks):
            outs[c * pieces + piece][:, place : place + TILE] = total[c * QUARTER : (c + 1) * QUARTER]


def product(up_rows, activations, pieces):
    rows, tokens = up_rows.shape
    width = activations.shape[2]
    count = rows // QUARTER * pieces
    return pl.pallas_call(
        product_kernel,
        in_specs=[IN_VMEM, IN_VMEM],
        out_specs=[IN_VMEM] * count,
        out_shape=[jax.ShapeDtypeStruct((QUARTER, width // pieces), BF16)] * count,
        compiler_params=SMALL,
        cost_estimate=pl.CostEstimate(
            flops=2 * rows * tokens * width,
            bytes_accessed=2 * tokens * (width + rows) + 2 * rows * width,
            transcendentals=0,
        ),
        name="product",
    )(up_rows, activations)


def add_first_kernel(own, left_one, left_two, right_one, right_two, *outs):
    half = left_one.shape[1]
    for h, (one, two) in enumerate(((left_one, left_two), (right_one, right_two))):
        cols = slice(h * half, (h + 1) * half)
        total = own[:, cols].astype(F32) + (one[...].astype(F32) + two[...].astype(F32))
        for j in range(4):
            outs[j][:, cols] = total[j * PAIR : (j + 1) * PAIR].astype(BF16)


def add_first(parts):
    return pl.pallas_call(
        add_first_kernel,
        out_shape=[jax.ShapeDtypeStruct((PAIR, parts[0].shape[1]), BF16)] * 4,
        compiler_params=SMALL,
        name="add_first",
    )(*parts)


def packed(rows):
    half = rows.shape[1] // 2
    return jnp.concatenate([rows[:, :half], rows[:, half:]], axis=0).astype(BF16)


def add_second_kernel(own, one, two, three, keep, away):
    total = (own[...].astype(F32) + one[...].astype(F32)) + (
        two[...].astype(F32) + three[...].astype(F32)
    )
    keep[...] = total[:OWN]
    away[...] = packed(total[OWN:])


def add_second(parts):
    width = parts[0].shape[1]
    return pl.pallas_call(
        add_second_kernel,
        out_shape=[
            jax.ShapeDtypeStruct((OWN, width), F32),
            jax.ShapeDtypeStruct((PAIR, width // 2), BF16),
        ],
        compiler_params=SMALL,
        name="add_second",
    )(*parts)


def inner_kernel(pos, keep, arrived, drift, first, second, base, exponents, first_out, second_out, own, away, unscale_out):
    _, core, _, _, _ = coordinates(pos)
    width = keep.shape[1]
    share = width // N_ISLAND
    per_share = share // BLOCK
    exponent = exponents[...].astype(F32)
    scaling_all = jnp.exp2(-exponent)
    unscale_all = jnp.exp2(exponent)

    def spread(values, i):
        return jnp.concatenate(
            [
                jnp.broadcast_to(values[:, b : b + 1], (OWN, BLOCK))
                for b in range(i * per_share, (i + 1) * per_share)
            ],
            axis=1,
        )

    def coded_share(i, received):
        cols = slice(i * share, (i + 1) * share)
        gradient = keep[:, cols] + received
        base_now = base[:, cols]
        params = base_now + drift[0, :, cols]
        first_new = BETA_FIRST * first[0, :, cols] + (1.0 - BETA_FIRST) * gradient
        second_new = BETA_SECOND * second[0, :, cols] + (1.0 - BETA_SECOND) * gradient * gradient
        first_out[0, :, cols] = first_new
        second_out[0, :, cols] = second_new
        update = (
            first_new / CORRECT_FIRST / (jnp.sqrt(second_new / CORRECT_SECOND) + EPSILON)
            + WEIGHT_DECAY * params
        )
        inner = params - INNER_RATE * update
        return jnp.clip((base_now - inner) * spread(scaling_all, i), -127.0, 127.0)

    for i in range(N_ISLAND // 2):
        received = arrived[:, i * share : (i + 1) * share].astype(F32)
        upper = coded_share(i, received[:OWN])
        lower = coded_share(i + N_ISLAND // 2, received[OWN:])
        coded = jnp.concatenate([upper, lower], axis=0).astype(BF16)
        place = slice((i // 2) * share, (i // 2 + 1) * share)
        place_lower = slice((i // 2 + 2) * share, (i // 2 + 3) * share)

        @pl.when(core == i % 2)
        def _():
            own[:, place] = coded
            unscale_out[:, place] = spread(unscale_all, i)
            unscale_out[:, place_lower] = spread(unscale_all, i + N_ISLAND // 2)

        @pl.when(core != i % 2)
        def _():
            away[:, place] = coded


def inner_step(pos, keep, arrived, drift, first, second, base, exponents):
    width = keep.shape[1]
    return pl.pallas_call(
        inner_kernel,
        in_specs=[SCALARS] + [IN_VMEM] * 7,
        out_specs=[IN_VMEM] * 5,
        out_shape=[
            jax.ShapeDtypeStruct(first.shape, F32),
            jax.ShapeDtypeStruct(second.shape, F32),
            jax.ShapeDtypeStruct((PAIR, width // 4), BF16),
            jax.ShapeDtypeStruct((PAIR, width // 4), BF16),
            jax.ShapeDtypeStruct((OWN, width // 2), F32),
        ],
        compiler_params=SMALL,
        name="inner_step",
    )(pos, keep, arrived, drift, first, second, base, exponents)


def add_two_kernel(own, arrived, out):
    out[...] = (own[...].astype(F32) + arrived[...].astype(F32)).astype(BF16)


def add_two(own, arrived):
    return pl.pallas_call(
        add_two_kernel,
        out_shape=jax.ShapeDtypeStruct(own.shape, BF16),
        compiler_params=SMALL,
        name="add_two",
    )(own, arrived)


def outer_kernel(pos, own, three, two, one, unscale, momentum, base, momentum_out, base_out, fragment):
    zlo, core, _, _, _ = coordinates(pos)
    share = own.shape[1] // 2

    def outer_share(k, summed):
        cols = pl.ds(pl.multiple_of((2 * k + core) * share, BLOCK), share)
        pseudo = summed * unscale[:, k * share : (k + 1) * share] / N_ISLAND
        momentum_next = NESTEROV_MU * momentum[:, cols] + pseudo
        base_next = base[:, cols] - OUTER_RATE * (pseudo + NESTEROV_MU * momentum_next)

        @pl.when(zlo == k)
        def _():
            momentum_out[...] = momentum_next
            base_out[...] = base_next

        return base_next

    for k in range(N_ZLO // 2):
        place = slice(k * share, (k + 1) * share)
        summed = (own[:, place].astype(F32) + one[:, place].astype(F32)) + (
            two[:, place].astype(F32) + three[:, place].astype(F32)
        )
        upper = outer_share(k, summed[:OWN])
        lower = outer_share(k + 2, summed[OWN:])
        fragment[:, place] = jnp.concatenate([upper, lower], axis=0).astype(BF16)


def outer_step(pos, parts, unscale, momentum, base):
    width = base.shape[1]
    return pl.pallas_call(
        outer_kernel,
        in_specs=[SCALARS] + [IN_VMEM] * 7,
        out_specs=[IN_VMEM] * 3,
        out_shape=[
            jax.ShapeDtypeStruct((OWN, width // N_ISLAND), F32),
            jax.ShapeDtypeStruct((OWN, width // N_ISLAND), F32),
            jax.ShapeDtypeStruct((PAIR, width // 4), BF16),
        ],
        compiler_params=SMALL,
        name="outer_step",
    )(pos, *parts, unscale, momentum, base)


def join_kernel(*refs):
    *parts, out = refs
    out[...] = jnp.concatenate([p[...].astype(F32) for p in parts], axis=0).astype(BF16)


def join(parts):
    rows, width = parts[0].shape
    return pl.pallas_call(
        join_kernel,
        out_shape=jax.ShapeDtypeStruct((len(parts) * rows, width), BF16),
        compiler_params=SMALL,
        name="join",
    )(*parts)


def place_kernel(w, pos, *refs):
    parts = refs[0], refs[1], refs[3], refs[2]
    out, held, sent = refs[-3:]
    _, core, zhi, y, x = coordinates(pos)
    whose = core if w == 0 else 1 - core
    line_rows = RING * OWN
    share = parts[0].shape[1] // 2

    def fill(a_is_x, x_here, k, b):
        source = pl.ds(pl.multiple_of(k * share + b * BLOCK, BLOCK), BLOCK)
        for q in range(RING):
            rows = []
            for x_there in range(RING):
                jx = (x_here - x_there) % RING
                ja, jb = (jx, q) if a_is_x else (q, jx)
                rows.append(parts[ja][jb * 2 * PAIR : (jb + 1) * 2 * PAIR, source].astype(F32))
            for jz in range(2):
                half = zhi if jz == 0 else 1 - zhi
                line = half * RING + lax.rem(y + RING - q, RING)
                start = pl.multiple_of(line * line_rows, 16)
                for h in range(2):
                    first = jz * PAIR + h * OWN
                    target = pl.ds(pl.multiple_of((2 * h + k) * share + b * BLOCK, BLOCK), BLOCK)
                    held[pl.ds(start, line_rows), target] = jnp.concatenate(
                        [r[first : first + OWN] for r in rows], axis=0
                    ).astype(BF16)

    copies = []
    for k in range(2):
        for a_is_x in (True, False):
            for x_here in range(RING):

                @pl.when(((whose == 0) == a_is_x) & (x == x_here))
                def _():
                    @pl.loop(0, share // BLOCK)
                    def _(b):
                        fill(a_is_x, x_here, k, b)

        for zlo in (k, 2 + k):
            cols = pl.ds(pl.multiple_of((2 * zlo + whose) * share, BLOCK), share)
            copies.append(
                pltpu.make_async_copy(
                    held.at[:, pl.ds(zlo * share, share)], out.at[:, cols], sent.at[len(copies)]
                )
            )
            copies[-1].start()
    for copy in copies:
        copy.wait()


def place(w, pos, parts, fragment=None):
    width = 4 * parts[0].shape[1]
    again = () if fragment is None else (fragment,)
    return pl.pallas_call(
        functools.partial(place_kernel, w),
        in_specs=[SCALARS] + [IN_VMEM] * 4 + [IN_HBM] * len(again),
        out_specs=IN_HBM,
        out_shape=jax.ShapeDtypeStruct((ROWS, width), BF16),
        scratch_shapes=[pltpu.VMEM((ROWS, width // 2), BF16), pltpu.SemaphoreType.DMA((4,))],
        input_output_aliases={5: 0} if again else {},
        compiler_params=SMALL,
        name="place",
    )(pos, *parts, *again)


def local(activations, upstream, drift, first_moment, second_moment, outer_base, outer_momentum, scale_exponents):
    pos = lax.axis_index(AXES).astype(jnp.int32).reshape(1)

    far_left, far_right, up_sides, up_own, activations = far_product(pos, upstream, activations)
    via_left = send(far_left, along_a(1))
    via_right = send(far_right, along_a(-1))
    next_left, next_right, last_left, last_right = product(up_sides, activations, 2)
    right_one = send(next_right, along_a(1))
    left_two = send(last_left, along_a(-1))
    (own,) = product(up_own, activations, 1)
    left_one = send(add_two(next_left, via_left), along_a(1))
    right_two = send(add_two(last_right, via_right), along_a(-1))
    chunks = add_first([own, left_one, left_two, right_one, right_two])
    keep, away = add_second([chunks[0]] + [send(chunks[j], along_b(j)) for j in (2, 1, 3)])
    arrived = send(away, OTHER_ZHI)

    first_new, second_new, own, away, unscale = inner_step(
        pos, keep, arrived, drift, first_moment, second_moment, outer_base, scale_exponents
    )
    coded = add_two(own, send(away, OTHER_CORE))
    parts = [send(coded, other_zlo(k)) for k in (3, 2, 1)]
    flat = (first_new.size // BLOCK, BLOCK)
    first_flat, second_flat, *parts = lax.optimization_barrier(
        (first_new.reshape(flat), second_new.reshape(flat), *parts)
    )
    momentum_out, base_out, piece = outer_step(pos, [coded, *parts], unscale, outer_momentum, outer_base)

    piece = join([piece, send(piece, NEAR_OTHER_ZHI)])
    line = {j: send(piece, along_b(-j)) for j in (2, 1, 3)}
    piece = join([piece, line[1], line[2], line[3]])
    plane = {j: send(piece, along_a(-j)) for j in (2, 1, 3)}
    mine = [piece, plane[1], plane[2], plane[3]]
    theirs = [send(m, OTHER_CORE) for m in mine]
    order = (0, 1, 3, 2)
    fragment = place(0, pos, [mine[j] for j in order])
    fragment = place(1, pos, [theirs[j] for j in order], fragment)
    return (
        first_flat.reshape(first_new.shape),
        second_flat.reshape(second_new.shape),
        momentum_out,
        base_out,
        fragment,
    )


def solution(mesh):
    in_specs = (
        P("island", "fsdp", None),
        P("island", "fsdp", None),
        P("island", "fsdp", None),
        P("island", "fsdp", None),
        P("island", "fsdp", None),
        P("fsdp", None),
        P("fsdp", None),
        P("fsdp", None),
    )
    out_specs = (
        P("island", "fsdp", None),
        P("island", "fsdp", None),
        P("fsdp", "island"),
        P("fsdp", "island"),
        P(),
    )
    return jax.shard_map(local, mesh=mesh, in_specs=in_specs, out_specs=out_specs, check_vma=False)
```

```python
import functools

import jax
import jax.numpy as jnp
import numpy as np
from jax import lax
from jax.experimental import pallas as pl
from jax.experimental.pallas import tpu as pltpu
from jax.sharding import PartitionSpec as P

INNER_RATE = 0.02
OUTER_RATE = 0.7
BETA_FIRST = 0.9
BETA_SECOND = 0.95
CORRECT_FIRST = 1.0 - 0.9**10
CORRECT_SECOND = 1.0 - 0.95**10
WEIGHT_DECAY = 0.1
EPSILON = 1e-08
NESTEROV_MU = 0.9

N_ISLAND = 8
N_FSDP = 32
N_ZLO = 4
RING = 4
OWN = 12
ROWS = 384
QUARTER = ROWS // 4
PAIR = 2 * OWN
BLOCK = 128
MIB = 1 << 20
BF16 = jnp.bfloat16
F32 = jnp.float32
TILE = 2560
READ_TILE = 2560
AHEAD = 2
AXES = ("island", "fsdp")
SCALARS = pl.BlockSpec(memory_space=pltpu.SMEM)
IN_VMEM = pl.BlockSpec(memory_space=pltpu.VMEM)
IN_HBM = pl.BlockSpec(memory_space=pltpu.HBM)
SMALL = pltpu.CompilerParams(vmem_limit_bytes=16 * MIB)


def device_pairs(target):
    pairs = []
    for zlo in range(N_ZLO):
        for core in range(2):
            for zhi in range(2):
                for y in range(RING):
                    for x in range(RING):
                        here = (zlo, core, zhi, y, x)
                        pairs.append((device_id(*here), device_id(*target(*here))))
    return pairs


def device_id(zlo, core, zhi, y, x):
    return (zlo * 2 + core) * N_FSDP + (zhi * RING + y) * RING + x


def along_a(step):
    def target(zlo, core, zhi, y, x):
        if core == 0:
            return (zlo, core, zhi, y, (x - step) % RING)
        return (zlo, core, zhi, (y - step) % RING, x)

    return device_pairs(target)


def along_b(step):
    def target(zlo, core, zhi, y, x):
        if core == 0:
            return (zlo, core, zhi, (y - step) % RING, x)
        return (zlo, core, zhi, y, (x - step) % RING)

    return device_pairs(target)


OTHER_ZHI = device_pairs(lambda zlo, core, zhi, y, x: (zlo, core, 1 - zhi, y, x))
NEAR_OTHER_ZHI = device_pairs(lambda zlo, core, zhi, y, x: (zlo ^ 2, core, 1 - zhi, y, x))
OTHER_CORE = device_pairs(lambda zlo, core, zhi, y, x: (zlo, 1 - core, zhi, y, x))


def other_zlo(k):
    return device_pairs(lambda zlo, core, zhi, y, x: (zlo ^ k, core, zhi, y, x))


def send(value, pairs):
    return lax.ppermute(value, AXES, pairs)


def coordinates(pos):
    device = pos[0]
    bit = lambda low, count: lax.bitwise_and(lax.shift_right_logical(device, jnp.int32(low)), jnp.int32(count - 1))
    return bit(6, N_ZLO), bit(5, 2), bit(4, 2), bit(2, RING), bit(0, RING)


def fragment_row(position, core, zhi, y, x):
    position = position.astype(F32)
    ja = jnp.floor((position + 0.5) / QUARTER)
    rest = position - QUARTER * ja
    jb = jnp.floor((rest + 0.5) / PAIR)
    rest = rest - PAIR * jb
    jz = jnp.floor((rest + 0.5) / OWN)
    r = rest - OWN * jz
    first = jnp.where(core == 0, ja, jb)
    second = jnp.where(core == 0, jb, ja)
    col = x.astype(F32) - first
    col = jnp.where(col < 0, col + RING, col)
    line = y.astype(F32) - second
    line = jnp.where(line < 0, line + RING, line)
    half = jnp.where(zhi == 0, jz, 1.0 - jz)
    return ((half * RING + line) * RING + col) * OWN + r


def far_kernel(pos, up_ref, act_ref, left, right, up_sides, up_own, act_held, up_held, up_arrived, arrived):
    up_copy = pltpu.make_async_copy(up_ref.at[0], up_held, up_arrived)
    up_copy.start()
    tiles = act_ref.shape[2] // READ_TILE
    copies = []
    for t in range(tiles):
        cols = pl.ds(t * READ_TILE, READ_TILE)
        copies.append(
            pltpu.make_async_copy(act_ref.at[0, :, cols], act_held.at[0, :, cols], arrived.at[t])
        )
    for copy in copies[:AHEAD]:
        copy.start()
    _, core, zhi, y, x = coordinates(pos)
    wanted = fragment_row(lax.broadcasted_iota(jnp.int32, (ROWS, 1), 0), core, zhi, y, x)
    column = lax.broadcasted_iota(jnp.int32, (ROWS, ROWS), 1).astype(F32)
    pick = jnp.where(column == wanted, 1.0, 0.0).astype(BF16)
    up_copy.wait()
    up_rows = lax.dot_general(
        pick, up_held[...], (((1,), (1,)), ((), ())), preferred_element_type=F32
    ).astype(BF16)
    up_own[...] = up_rows[:QUARTER]
    up_sides[:QUARTER] = up_rows[QUARTER : 2 * QUARTER]
    up_sides[QUARTER:] = up_rows[3 * QUARTER :]
    up_far = up_rows[2 * QUARTER : 3 * QUARTER]
    half = left.shape[1]
    for t in range(tiles):
        copies[t].wait()
        if t + AHEAD < tiles:
            copies[t + AHEAD].start()
        first = t * READ_TILE
        out, place = (left, first) if first < half else (right, first - half)
        out[:, place : place + READ_TILE] = jnp.dot(
            up_far, act_held[0, :, first : first + READ_TILE], preferred_element_type=F32
        ).astype(BF16)


def far_product(pos, upstream, activations):
    _, tokens, width = activations.shape
    shapes = [
        (QUARTER, width // 2),
        (QUARTER, width // 2),
        (2 * QUARTER, tokens),
        (QUARTER, tokens),
        activations.shape,
    ]
    return pl.pallas_call(
        far_kernel,
        in_specs=[SCALARS, IN_HBM, IN_HBM],
        out_specs=[IN_VMEM] * 5,
        out_shape=[jax.ShapeDtypeStruct(shape, BF16) for shape in shapes],
        scratch_shapes=[
            pltpu.VMEM((tokens, ROWS), BF16),
            pltpu.SemaphoreType.DMA,
            pltpu.SemaphoreType.DMA((width // READ_TILE,)),
        ],
        compiler_params=SMALL,
        name="far_product",
    )(
        pos,
        pltpu.with_memory_space_constraint(upstream, pltpu.HBM),
        pltpu.with_memory_space_constraint(activations, pltpu.HBM),
    )


def product_kernel(up_rows, act_ref, *outs):
    width = act_ref.shape[2]
    chunks = up_rows.shape[0] // QUARTER
    pieces = len(outs) // chunks
    per_out = width // pieces
    for first in range(0, width, TILE):
        total = jnp.dot(
            up_rows[...], act_ref[0, :, first : first + TILE], preferred_element_type=F32
        ).astype(BF16)
        piece, place = divmod(first, per_out)
        for c in range(chunks):
            outs[c * pieces + piece][:, place : place + TILE] = total[c * QUARTER : (c + 1) * QUARTER]


def product(up_rows, activations, pieces):
    rows, tokens = up_rows.shape
    width = activations.shape[2]
    count = rows // QUARTER * pieces
    return pl.pallas_call(
        product_kernel,
        in_specs=[IN_VMEM, IN_VMEM],
        out_specs=[IN_VMEM] * count,
        out_shape=[jax.ShapeDtypeStruct((QUARTER, width // pieces), BF16)] * count,
        compiler_params=SMALL,
        cost_estimate=pl.CostEstimate(
            flops=2 * rows * tokens * width,
            bytes_accessed=2 * tokens * (width + rows) + 2 * rows * width,
            transcendentals=0,
        ),
        name="product",
    )(up_rows, activations)


def add_first_kernel(own, left_one, left_two, right_one, right_two, *outs):
    half = left_one.shape[1]
    for h, (one, two) in enumerate(((left_one, left_two), (right_one, right_two))):
        cols = slice(h * half, (h + 1) * half)
        total = own[:, cols].astype(F32) + (one[...].astype(F32) + two[...].astype(F32))
        for j in range(4):
            outs[j][:, cols] = total[j * PAIR : (j + 1) * PAIR].astype(BF16)


def add_first(parts):
    return pl.pallas_call(
        add_first_kernel,
        out_shape=[jax.ShapeDtypeStruct((PAIR, parts[0].shape[1]), BF16)] * 4,
        compiler_params=SMALL,
        name="add_first",
    )(*parts)


def packed(rows):
    half = rows.shape[1] // 2
    return jnp.concatenate([rows[:, :half], rows[:, half:]], axis=0).astype(BF16)


def add_second_kernel(own, one, two, three, keep, away):
    total = (own[...].astype(F32) + one[...].astype(F32)) + (
        two[...].astype(F32) + three[...].astype(F32)
    )
    keep[...] = total[:OWN]
    away[...] = packed(total[OWN:])


def add_second(parts):
    width = parts[0].shape[1]
    return pl.pallas_call(
        add_second_kernel,
        out_shape=[
            jax.ShapeDtypeStruct((OWN, width), F32),
            jax.ShapeDtypeStruct((PAIR, width // 2), BF16),
        ],
        compiler_params=SMALL,
        name="add_second",
    )(*parts)


def inner_kernel(pos, keep, arrived, drift, first, second, base, exponents, first_out, second_out, own, away, unscale_out):
    _, core, _, _, _ = coordinates(pos)
    width = keep.shape[1]
    share = width // N_ISLAND
    per_share = share // BLOCK
    exponent = exponents[...].astype(F32)
    scaling_all = jnp.exp2(-exponent)
    unscale_all = jnp.exp2(exponent)

    def spread(values, i):
        return jnp.concatenate(
            [
                jnp.broadcast_to(values[:, b : b + 1], (OWN, BLOCK))
                for b in range(i * per_share, (i + 1) * per_share)
            ],
            axis=1,
        )

    def coded_share(i, received):
        cols = slice(i * share, (i + 1) * share)
        gradient = keep[:, cols] + received
        base_now = base[:, cols]
        params = base_now + drift[0, :, cols]
        first_new = BETA_FIRST * first[0, :, cols] + (1.0 - BETA_FIRST) * gradient
        second_new = BETA_SECOND * second[0, :, cols] + (1.0 - BETA_SECOND) * gradient * gradient
        first_out[0, :, cols] = first_new
        second_out[0, :, cols] = second_new
        update = (
            first_new / CORRECT_FIRST / (jnp.sqrt(second_new / CORRECT_SECOND) + EPSILON)
            + WEIGHT_DECAY * params
        )
        inner = params - INNER_RATE * update
        return jnp.clip((base_now - inner) * spread(scaling_all, i), -127.0, 127.0)

    for i in range(N_ISLAND // 2):
        received = arrived[:, i * share : (i + 1) * share].astype(F32)
        upper = coded_share(i, received[:OWN])
        lower = coded_share(i + N_ISLAND // 2, received[OWN:])
        coded = jnp.concatenate([upper, lower], axis=0).astype(BF16)
        place = slice((i // 2) * share, (i // 2 + 1) * share)
        place_lower = slice((i // 2 + 2) * share, (i // 2 + 3) * share)

        @pl.when(core == i % 2)
        def _():
            own[:, place] = coded
            unscale_out[:, place] = spread(unscale_all, i)
            unscale_out[:, place_lower] = spread(unscale_all, i + N_ISLAND // 2)

        @pl.when(core != i % 2)
        def _():
            away[:, place] = coded


def inner_step(pos, keep, arrived, drift, first, second, base, exponents):
    width = keep.shape[1]
    return pl.pallas_call(
        inner_kernel,
        in_specs=[SCALARS] + [IN_VMEM] * 7,
        out_specs=[IN_VMEM] * 5,
        out_shape=[
            jax.ShapeDtypeStruct(first.shape, F32),
            jax.ShapeDtypeStruct(second.shape, F32),
            jax.ShapeDtypeStruct((PAIR, width // 4), BF16),
            jax.ShapeDtypeStruct((PAIR, width // 4), BF16),
            jax.ShapeDtypeStruct((OWN, width // 2), F32),
        ],
        compiler_params=SMALL,
        name="inner_step",
    )(pos, keep, arrived, drift, first, second, base, exponents)


def add_two_kernel(own, arrived, out):
    out[...] = (own[...].astype(F32) + arrived[...].astype(F32)).astype(BF16)


def add_two(own, arrived):
    return pl.pallas_call(
        add_two_kernel,
        out_shape=jax.ShapeDtypeStruct(own.shape, BF16),
        compiler_params=SMALL,
        name="add_two",
    )(own, arrived)


def outer_kernel(pos, own, two, three, one, unscale, momentum, base, momentum_out, base_out, fragment):
    zlo, core, _, _, _ = coordinates(pos)
    share = own.shape[1] // 2

    def outer_share(k, summed):
        cols = pl.ds(pl.multiple_of((2 * k + core) * share, BLOCK), share)
        pseudo = summed * unscale[:, k * share : (k + 1) * share] / N_ISLAND
        momentum_next = NESTEROV_MU * momentum[:, cols] + pseudo
        base_next = base[:, cols] - OUTER_RATE * (pseudo + NESTEROV_MU * momentum_next)

        @pl.when(zlo == k)
        def _():
            momentum_out[...] = momentum_next
            base_out[...] = base_next

        return base_next

    for k in range(N_ZLO // 2):
        place = slice(k * share, (k + 1) * share)
        summed = (own[:, place].astype(F32) + one[:, place].astype(F32)) + (
            two[:, place].astype(F32) + three[:, place].astype(F32)
        )
        upper = outer_share(k, summed[:OWN])
        lower = outer_share(k + 2, summed[OWN:])
        fragment[:, place] = jnp.concatenate([upper, lower], axis=0).astype(BF16)


def outer_step(pos, parts, unscale, momentum, base):
    width = base.shape[1]
    return pl.pallas_call(
        outer_kernel,
        in_specs=[SCALARS] + [IN_VMEM] * 7,
        out_specs=[IN_VMEM] * 3,
        out_shape=[
            jax.ShapeDtypeStruct((OWN, width // N_ISLAND), F32),
            jax.ShapeDtypeStruct((OWN, width // N_ISLAND), F32),
            jax.ShapeDtypeStruct((PAIR, width // 4), BF16),
        ],
        compiler_params=SMALL,
        name="outer_step",
    )(pos, *parts, unscale, momentum, base)


def join_kernel(*refs):
    *parts, out = refs
    out[...] = jnp.concatenate([p[...].astype(F32) for p in parts], axis=0).astype(BF16)


def join(parts):
    rows, width = parts[0].shape
    return pl.pallas_call(
        join_kernel,
        out_shape=jax.ShapeDtypeStruct((len(parts) * rows, width), BF16),
        compiler_params=SMALL,
        name="join",
    )(*parts)


def place_kernel(w, pos, *refs):
    parts = refs[0], refs[1], refs[3], refs[2]
    out, held, sent = refs[-3:]
    _, core, zhi, y, x = coordinates(pos)
    whose = core if w == 0 else 1 - core
    line_rows = RING * OWN
    share = parts[0].shape[1] // 2

    def fill(a_is_x, x_here, k, b):
        source = pl.ds(pl.multiple_of(k * share + b * BLOCK, BLOCK), BLOCK)
        for q in range(RING):
            rows = []
            for x_there in range(RING):
                jx = (x_here - x_there) % RING
                ja, jb = (jx, q) if a_is_x else (q, jx)
                rows.append(parts[ja][jb * 2 * PAIR : (jb + 1) * 2 * PAIR, source].astype(F32))
            for jz in range(2):
                half = zhi if jz == 0 else 1 - zhi
                line = half * RING + lax.rem(y + RING - q, RING)
                start = pl.multiple_of(line * line_rows, 16)
                for h in range(2):
                    first = jz * PAIR + h * OWN
                    target = pl.ds(pl.multiple_of((2 * h + k) * share + b * BLOCK, BLOCK), BLOCK)
                    held[pl.ds(start, line_rows), target] = jnp.concatenate(
                        [r[first : first + OWN] for r in rows], axis=0
                    ).astype(BF16)

    copies = []
    for k in range(2):
        for a_is_x in (True, False):
            for x_here in range(RING):

                @pl.when(((whose == 0) == a_is_x) & (x == x_here))
                def _():
                    @pl.loop(0, share // BLOCK)
                    def _(b):
                        fill(a_is_x, x_here, k, b)

        for zlo in (k, 2 + k):
            cols = pl.ds(pl.multiple_of((2 * zlo + whose) * share, BLOCK), share)
            copies.append(
                pltpu.make_async_copy(
                    held.at[:, pl.ds(zlo * share, share)], out.at[:, cols], sent.at[len(copies)]
                )
            )
            copies[-1].start()
    for copy in copies:
        copy.wait()


def place(w, pos, parts, fragment=None):
    width = 4 * parts[0].shape[1]
    again = () if fragment is None else (fragment,)
    return pl.pallas_call(
        functools.partial(place_kernel, w),
        in_specs=[SCALARS] + [IN_VMEM] * 4 + [IN_HBM] * len(again),
        out_specs=IN_HBM,
        out_shape=jax.ShapeDtypeStruct((ROWS, width), BF16),
        scratch_shapes=[pltpu.VMEM((ROWS, width // 2), BF16), pltpu.SemaphoreType.DMA((4,))],
        input_output_aliases={5: 0} if again else {},
        compiler_params=SMALL,
        name="place",
    )(pos, *parts, *again)


def local(activations, upstream, drift, first_moment, second_moment, outer_base, outer_momentum, scale_exponents):
    pos = lax.axis_index(AXES).astype(jnp.int32).reshape(1)

    far_left, far_right, up_sides, up_own, activations = far_product(pos, upstream, activations)
    via_left = send(far_left, along_a(1))
    via_right = send(far_right, along_a(-1))
    next_left, next_right, last_left, last_right = product(up_sides, activations, 2)
    right_one = send(next_right, along_a(1))
    left_two = send(last_left, along_a(-1))
    (own,) = product(up_own, activations, 1)
    left_one = send(add_two(next_left, via_left), along_a(1))
    right_two = send(add_two(last_right, via_right), along_a(-1))
    chunks = add_first([own, left_one, left_two, right_one, right_two])
    keep, away = add_second([chunks[0]] + [send(chunks[j], along_b(j)) for j in (2, 1, 3)])
    arrived = send(away, OTHER_ZHI)

    first_new, second_new, own, away, unscale = inner_step(
        pos, keep, arrived, drift, first_moment, second_moment, outer_base, scale_exponents
    )
    coded = add_two(own, send(away, OTHER_CORE))
    parts = [send(coded, other_zlo(k)) for k in (2, 3, 1)]
    flat = (first_new.size // BLOCK, BLOCK)
    first_flat, second_flat, *parts = lax.optimization_barrier(
        (first_new.reshape(flat), second_new.reshape(flat), *parts)
    )
    momentum_out, base_out, piece = outer_step(pos, [coded, *parts], unscale, outer_momentum, outer_base)

    piece = join([piece, send(piece, NEAR_OTHER_ZHI)])
    line = {j: send(piece, along_b(-j)) for j in (2, 1, 3)}
    piece = join([piece, line[1], line[2], line[3]])
    plane = {j: send(piece, along_a(-j)) for j in (2, 1, 3)}
    mine = [piece, plane[1], plane[2], plane[3]]
    theirs = [send(m, OTHER_CORE) for m in mine]
    order = (0, 1, 3, 2)
    fragment = place(0, pos, [mine[j] for j in order])
    fragment = place(1, pos, [theirs[j] for j in order], fragment)
    return (
        first_flat.reshape(first_new.shape),
        second_flat.reshape(second_new.shape),
        momentum_out,
        base_out,
        fragment,
    )


def solution(mesh):
    in_specs = (
        P("island", "fsdp", None),
        P("island", "fsdp", None),
        P("island", "fsdp", None),
        P("island", "fsdp", None),
        P("island", "fsdp", None),
        P("fsdp", None),
        P("fsdp", None),
        P("fsdp", None),
    )
    out_specs = (
        P("island", "fsdp", None),
        P("island", "fsdp", None),
        P("fsdp", "island"),
        P("fsdp", "island"),
        P(),
    )
    return jax.shard_map(local, mesh=mesh, in_specs=in_specs, out_specs=out_specs, check_vma=False)
```
